32 devices in a mesh: tile: 8 (over y, x, core), view: 4 (over z).
Axes of the slice: x: 2, y: 2, z: 4, core: 2. Of those that a mesh axis runs over, the one named last changes fastest.
Arguments:
- initial: float32 [8, 4, 256, 256], P('tile'), may hold values from 0.5 to 2
- recorded: float32 [4, 8, 4, 256, 256], P('view', 'tile'), may hold values from 0.2 to 3
- tap_table: float32 [4, 8, 3, 31], P('view'), may hold values from 0.02 to 1
- variants: int32 [4, 8], P('view'), may hold values from 0 to 7
Outputs:
- estimate: float32 [8, 4, 256, 256], P('tile')
The draws below stay inside these ranges and needn't reach their ends.
Inputs may be any that keep to these rules, and one draw needn't show every extreme that they name: `variants`: indices of the 8 tap tables of the view.
All inputs are finite; a program needn't handle non-finite values.
Results may differ from the reference program's by a relative error of at most 0.0001.
Values sent between devices are 32-bit elements; how exact they have to be, the bound alone decides.
A program may use at most 192 MiB of HBM per device.

```python
import math
import jax
import jax.numpy as jnp
from jax import lax

Z = 4
TY = 256
TX = 256
GX = 8
TAPS = 31
VARIANTS = 8
ITERS = 2
HALF = 15
VIEWS = 4
N_TILE = 8
N_VIEW = 4


def place_ends(values, own_key, smallest, largest):
    longest = values.shape.index(max(values.shape))
    spots = []
    for shift in (0, 1):
        where = [jax.random.randint(jax.random.fold_in(own_key, axis), (), 0, length) for axis, length in enumerate(values.shape)]
        where[longest] = (where[longest] + shift) % values.shape[longest]
        spots.append(tuple(where))
    return values.at[spots[0]].set(smallest).at[spots[1]].set(largest)


def levels(stream_key, dims, cuts, low, high):
    level = 1.0
    for position, shards_of in cuts:
        draws = jax.random.uniform(jax.random.fold_in(jax.random.fold_in(stream_key, 6), position), (shards_of,), jnp.float32, low / len(cuts), high / len(cuts))
        level = level * jnp.repeat(jnp.exp(draws), dims[position] // shards_of).reshape((-1,) + (1,) * (len(dims) - 1 - position))
    return level


def setup_inputs(seed: int = 0) -> dict:
    key_of = jax.random.split(jax.random.key(seed), 5)
    return {
        "initial": jnp.clip(0.5 + 1.5 * jax.random.uniform(key_of[0], (N_TILE, Z, TY, TX), jnp.float32) ** levels(key_of[0], (N_TILE, Z, TY, TX), ((0, 8),), -0.2, 0.2), 0.5, 2.0),
        "recorded": jnp.clip(0.2 + 2.8 * jax.random.uniform(key_of[1], (VIEWS, N_TILE, Z, TY, TX), jnp.float32) ** levels(key_of[1], (VIEWS, N_TILE, Z, TY, TX), ((0, 4), (1, 8)), -0.2, 0.2), 0.2, 3.0),
        "tap_table": jnp.clip(jnp.exp(math.log(1.0) - 3.912023 * jax.random.uniform(key_of[2], (VIEWS, VARIANTS, 3, TAPS), jnp.float32) ** levels(key_of[2], (VIEWS, VARIANTS, 3, TAPS), ((0, 4),), -0.2, 0.2)), 0.02, 1.0),
        "variants": place_ends(jax.random.randint(key_of[3], (VIEWS, N_TILE), 0, VARIANTS), jax.random.fold_in(key_of[3], 1), 0, VARIANTS - 1).astype(jnp.int32),
    }


def normalized(tap_table):
    return tap_table / jnp.sum(tap_table, axis=-1, keepdims=True)


def tile_kernels(kernels, variant_ids, grid_rows, grid_cols):
    count_variants = kernels.shape[0]
    onehot = (variant_ids[:, None] == jnp.arange(count_variants, dtype=jnp.int32)[None, :]).astype(jnp.float32)
    flat = jnp.dot(onehot, kernels.reshape(count_variants, -1), precision=lax.Precision.HIGHEST)
    return flat.reshape(grid_rows, grid_cols, 3, kernels.shape[-1])


def tile_onehot(positions, extent, count):
    owner = jnp.clip(jnp.floor_divide(positions, extent), 0, count - 1).astype(jnp.int32)
    return (owner[:, None] == jnp.arange(count, dtype=jnp.int32)[None, :]).astype(jnp.float32)


def weight_map(tile_taps, axis_id, offset, row_hot, col_hot):
    inner = jnp.dot(row_hot, tile_taps[:, :, axis_id, offset], precision=lax.Precision.HIGHEST)
    return jnp.dot(inner, col_hot.T, precision=lax.Precision.HIGHEST)


def blur_cols(padded, tile_taps, row_hot, col_hot):
    count = col_hot.shape[0]
    result = jnp.zeros((padded.shape[0], padded.shape[1], count), jnp.float32)
    for offset in range(tile_taps.shape[3]):
        weights = weight_map(tile_taps, 0, offset, row_hot, col_hot)
        result = result + weights[None] * padded[:, :, offset:offset + count]
    return result


def blur_rows(padded, tile_taps, row_hot, col_hot):
    count = row_hot.shape[0]
    result = jnp.zeros((padded.shape[0], count, padded.shape[2]), jnp.float32)
    for offset in range(tile_taps.shape[3]):
        weights = weight_map(tile_taps, 1, offset, row_hot, col_hot)
        result = result + weights[None] * padded[:, offset:offset + count, :]
    return result


def blur_planes(field, tile_taps, row_hot, col_hot, reverse):
    taps = tile_taps.shape[3]
    margin = taps // 2
    padded = jnp.pad(field, ((margin, margin), (0, 0), (0, 0)))
    planes = field.shape[0]
    result = jnp.zeros(field.shape, jnp.float32)
    for offset in range(taps):
        which = taps - 1 - offset if reverse else offset
        weights = weight_map(tile_taps, 2, which, row_hot, col_hot)
        result = result + weights[None] * padded[offset:offset + planes]
    return result


def adjoint_rows(padded, tile_taps, row_hot, col_hot):
    margin = tile_taps.shape[3] // 2
    count = padded.shape[1] - 2 * margin
    result = jnp.zeros((padded.shape[0], count, padded.shape[2]), jnp.float32)
    for offset in range(tile_taps.shape[3]):
        lead = 2 * margin - offset
        weights = weight_map(tile_taps, 1, offset, row_hot, col_hot)
        result = result + weights[None, lead:lead + count, :] * padded[:, lead:lead + count, :]
    return result


def adjoint_cols(padded, tile_taps, row_hot, col_hot):
    margin = tile_taps.shape[3] // 2
    count = padded.shape[2] - 2 * margin
    result = jnp.zeros((padded.shape[0], padded.shape[1], count), jnp.float32)
    for offset in range(tile_taps.shape[3]):
        lead = 2 * margin - offset
        weights = weight_map(tile_taps, 0, offset, row_hot, col_hot)
        result = result + weights[None, :, lead:lead + count] * padded[:, :, lead:lead + count]
    return result


def assemble(blocks, grid_rows):
    shaped = blocks.reshape(grid_rows, GX, Z, TY, TX)
    return shaped.transpose(2, 0, 3, 1, 4).reshape(Z, grid_rows * TY, GX * TX)


def disassemble(field, grid_rows):
    shaped = field.reshape(Z, grid_rows, TY, GX, TX)
    return shaped.transpose(1, 3, 0, 2, 4).reshape(grid_rows * GX, Z, TY, TX)


def reference(initial, recorded, tap_table, variants):
    grid_rows = N_TILE // GX
    estimate = assemble(initial, grid_rows)
    count_rows = grid_rows * TY
    count_cols = GX * TX
    own_rows = tile_onehot(jnp.arange(count_rows, dtype=jnp.int32), TY, grid_rows)
    own_cols = tile_onehot(jnp.arange(count_cols, dtype=jnp.int32), TX, GX)
    wide_rows = tile_onehot(jnp.arange(count_rows + 2 * HALF, dtype=jnp.int32) - HALF, TY, grid_rows)
    wide_cols = tile_onehot(jnp.arange(count_cols + 2 * HALF, dtype=jnp.int32) - HALF, TX, GX)
    for step in range(ITERS):
        logged = jnp.zeros(estimate.shape, jnp.float32)
        for view in range(N_VIEW):
            tile_taps = tile_kernels(normalized(tap_table[view]), variants[view], grid_rows, GX)
            observed = assemble(recorded[view], grid_rows)
            padded = jnp.pad(estimate, ((0, 0), (0, 0), (HALF, HALF)))
            planes = blur_planes(blur_cols(padded, tile_taps, own_rows, own_cols), tile_taps, own_rows, own_cols, False)
            blurred = blur_rows(jnp.pad(planes, ((0, 0), (HALF, HALF), (0, 0))), tile_taps, own_rows, own_cols)
            ratio = observed / blurred
            back = adjoint_rows(jnp.pad(ratio, ((0, 0), (HALF, HALF), (0, 0))), tile_taps, wide_rows, own_cols)
            back = blur_planes(back, tile_taps, own_rows, own_cols, True)
            correction = adjoint_cols(jnp.pad(back, ((0, 0), (0, 0), (HALF, HALF))), tile_taps, own_rows, wide_cols)
            logged = logged + jnp.log(correction)
        estimate = estimate * jnp.exp(logged / N_VIEW)
    return disassemble(estimate, grid_rows)
```

```python
import jax
import jax.numpy as jnp
from jax import lax
from jax.experimental import pallas as pl
from jax.experimental.pallas import tpu as pltpu
from jax.sharding import PartitionSpec as P

GX = 8
ITERS = 2
HALF = 15
EDGE = 16
MESH = pl.DeviceIdType.MESH


def passed_along(block, axis, distance):
    devices = range(lax.axis_size(axis))
    route = [(i - distance, i) for i in devices if i - distance in devices]
    return lax.ppermute(block, axis, route)


def normalized(tap_table):
    return tap_table / jnp.sum(tap_table, axis=-1, keepdims=True)


def tile_kernels(kernels, variant_ids, grid_rows, grid_cols):
    count_variants = kernels.shape[0]
    onehot = (variant_ids[:, None] == jnp.arange(count_variants, dtype=jnp.int32)[None, :]).astype(
        jnp.float32
    )
    flat = jnp.dot(onehot, kernels.reshape(count_variants, -1), precision=lax.Precision.HIGHEST)
    return flat.reshape(grid_rows, grid_cols, 3, kernels.shape[-1])


def tile_onehot(positions, extent, count):
    owner = jnp.clip(jnp.floor_divide(positions, extent), 0, count - 1)
    return (owner[:, None] == jnp.arange(count, dtype=jnp.int32)[None, :]).astype(jnp.float32)


def weight_map(tile_taps, axis_id, offset, row_hot, col_hot):
    inner = jnp.dot(row_hot, tile_taps[:, :, axis_id, offset], precision=lax.Precision.HIGHEST)
    return jnp.dot(inner, col_hot.T, precision=lax.Precision.HIGHEST)


def blur_cols(padded, tile_taps, row_hot, col_hot):
    count = col_hot.shape[0]
    result = jnp.zeros((padded.shape[0], padded.shape[1], count), jnp.float32)
    for offset in range(tile_taps.shape[3]):
        weights = weight_map(tile_taps, 0, offset, row_hot, col_hot)
        result = result + weights[None] * padded[:, :, offset : offset + count]
    return result


def blur_rows(padded, tile_taps, row_hot, col_hot):
    count = row_hot.shape[0]
    result = jnp.zeros((padded.shape[0], count, padded.shape[2]), jnp.float32)
    for offset in range(tile_taps.shape[3]):
        weights = weight_map(tile_taps, 1, offset, row_hot, col_hot)
        result = result + weights[None] * padded[:, offset : offset + count, :]
    return result


def blur_planes(field, tile_taps, row_hot, col_hot, reverse):
    taps = tile_taps.shape[3]
    margin = taps // 2
    padded = jnp.pad(field, ((margin, margin), (0, 0), (0, 0)))
    planes = field.shape[0]
    result = jnp.zeros(field.shape, jnp.float32)
    for offset in range(taps):
        which = taps - 1 - offset if reverse else offset
        weights = weight_map(tile_taps, 2, which, row_hot, col_hot)
        result = result + weights[None] * padded[offset : offset + planes]
    return result


def adjoint_rows(padded, tile_taps, row_hot, col_hot):
    margin = tile_taps.shape[3] // 2
    count = padded.shape[1] - 2 * margin
    result = jnp.zeros((padded.shape[0], count, padded.shape[2]), jnp.float32)
    for offset in range(tile_taps.shape[3]):
        lead = 2 * margin - offset
        weights = weight_map(tile_taps, 1, offset, row_hot, col_hot)
        result = result + weights[None, lead : lead + count, :] * padded[:, lead : lead + count, :]
    return result


def adjoint_cols(padded, tile_taps, row_hot, col_hot):
    margin = tile_taps.shape[3] // 2
    count = padded.shape[2] - 2 * margin
    result = jnp.zeros((padded.shape[0], padded.shape[1], count), jnp.float32)
    for offset in range(tile_taps.shape[3]):
        lead = 2 * margin - offset
        weights = weight_map(tile_taps, 0, offset, row_hot, col_hot)
        result = result + weights[None, :, lead : lead + count] * padded[:, :, lead : lead + count]
    return result


def widen_cols(field, width, tile_col):
    west_send = field[:, :, -width:]
    east_send = field[:, :, :width]
    west_send = jnp.where(tile_col < GX - 1, west_send, jnp.zeros_like(west_send))
    east_send = jnp.where(tile_col > 0, east_send, jnp.zeros_like(east_send))
    from_west = passed_along(west_send, "tile", 1)
    from_east = passed_along(east_send, "tile", -1)
    return jnp.concatenate([from_west, field, from_east], axis=2)


def widen_rows(field, width):
    from_north = passed_along(field[:, -width:, :], "tile", GX)
    from_south = passed_along(field[:, :width, :], "tile", -GX)
    return jnp.concatenate([from_north, field, from_south], axis=1)


def per_device(initial, recorded, tap_table, variants):
    position = lax.axis_index("tile")
    count_tiles = lax.axis_size("tile")
    count_views = lax.axis_size("view")
    grid_rows = count_tiles // GX
    tile_row = position // GX
    tile_col = position % GX
    tile_taps = tile_kernels(normalized(tap_table[0]), variants[0], grid_rows, GX)
    estimate = initial[0]
    observed = recorded[0, 0]
    tall = estimate.shape[1]
    broad = estimate.shape[2]
    row_first = tile_row * tall
    col_first = tile_col * broad

    def row_places(margin):
        return row_first + jnp.arange(tall + 2 * margin, dtype=jnp.int32) - margin

    def col_places(margin):
        return col_first + jnp.arange(broad + 2 * margin, dtype=jnp.int32) - margin

    own_rows = tile_onehot(row_places(0), tall, grid_rows)
    own_cols = tile_onehot(col_places(0), broad, GX)
    wide_rows = tile_onehot(row_places(HALF), tall, grid_rows)
    wide_cols = tile_onehot(col_places(HALF), broad, GX)
    for step in range(ITERS):
        padded = widen_cols(estimate, HALF, tile_col)
        planes = blur_planes(
            blur_cols(padded, tile_taps, own_rows, own_cols), tile_taps, own_rows, own_cols, False
        )
        blurred = blur_rows(widen_rows(planes, HALF), tile_taps, own_rows, own_cols)
        ratio = observed / blurred
        back = adjoint_rows(widen_rows(ratio, HALF), tile_taps, wide_rows, own_cols)
        back = blur_planes(back, tile_taps, own_rows, own_cols, True)
        correction = adjoint_cols(widen_cols(back, HALF, tile_col), tile_taps, own_rows, wide_cols)
        logged = jnp.log(correction)
        summed = lax.psum(logged, "view")
        estimate = estimate * jnp.exp(summed / count_views)
    return estimate[None]


def split(value):
    high = value.astype(jnp.bfloat16)
    return high, (value - high.astype(jnp.float32)).astype(jnp.bfloat16)


def product(left, right, contract):
    dims = (((contract[0],), (contract[1],)), ((), ()))

    def one(a, b):
        return lax.dot_general(a, b, dims, preferred_element_type=jnp.float32)

    return one(left[0], right[0]) + (one(left[0], right[1]) + one(left[1], right[0]))


def strips_kernel(
    init_ref,
    rec_ref,
    tap_ref,
    var_ref,
    out_ref,
    wide_ref,
    flip_ref,
    seen_ref,
    taps_ref,
    g_hi,
    g_lo,
    gt_hi,
    gt_lo,
    m_hi,
    m_lo,
    p_hi,
    p_lo,
    blur_ref,
    corr_ref,
    west_ref,
    east_ref,
    next_ref,
    tap_send,
    tap_recv,
    rec_send,
    rec_recv,
    edge_send,
    edge_recv,
    over_send,
    over_recv,
    halo_send,
    halo_recv,
    out_send,
    out_recv,
):
    tile = lax.axis_index("tile")
    view = lax.axis_index("view")
    tiles = lax.axis_size("tile")
    views = lax.axis_size("view")
    depth, tall, broad = init_ref.shape[1:]
    strip = broad // views
    span = strip + 2 * EDGE
    inner, outer = depth * strip, depth * span
    taps = tap_ref.shape[3]

    def strip_of(position):
        odd = lax.rem(tile, 2)
        return position + odd * (views - 1 - 2 * position)

    mine = strip_of(view)
    has_west = (tile > 0) | (mine > 0)
    has_east = (tile < tiles - 1) | (mine < views - 1)
    step = 1 - 2 * lax.rem(tile, 2)
    west_id = {
        "tile": jnp.where(mine > 0, tile, tile - 1),
        "view": jnp.where(mine > 0, view - step, view),
    }
    east_id = {
        "tile": jnp.where(mine < views - 1, tile, tile + 1),
        "view": jnp.where(mine < views - 1, view + step, view),
    }
    first = pl.multiple_of(mine * strip, strip)

    def peer(shift):
        other = lax.rem(view + shift, views)
        return other, {"tile": tile, "view": other}

    def copy(source, target, send, recv, device):
        return pltpu.make_async_remote_copy(
            src_ref=source,
            dst_ref=target,
            send_sem=send,
            recv_sem=recv,
            device_id=device,
            device_id_type=MESH,
        )

    barrier = pltpu.get_barrier_semaphore()
    for shift in range(1, views):
        pl.semaphore_signal(barrier, inc=1, device_id=peer(shift)[1], device_id_type=MESH)

    @pl.when(tile > 0)
    def _():
        pl.semaphore_signal(
            barrier, inc=1, device_id={"tile": tile - 1, "view": view}, device_id_type=MESH
        )

    @pl.when(tile < tiles - 1)
    def _():
        pl.semaphore_signal(
            barrier, inc=1, device_id={"tile": tile + 1, "view": view}, device_id_type=MESH
        )

    own_taps = tap_ref[0, var_ref[0, tile]]
    own_taps = own_taps / jnp.sum(own_taps, axis=-1, keepdims=True)
    taps_ref[view] = jnp.zeros(taps_ref.shape[1:], jnp.float32)
    taps_ref[view, 0:3, 0:taps] = own_taps
    flip_ref[0] = rec_ref[0, 0, 0].T

    pl.semaphore_wait(
        barrier, views - 1 + jnp.where(tile > 0, 1, 0) + jnp.where(tile < tiles - 1, 1, 0)
    )

    def tap_copy(shift):
        return copy(
            taps_ref.at[view],
            taps_ref.at[view],
            tap_send.at[shift - 1],
            tap_recv.at[view],
            peer(shift)[1],
        )

    for shift in range(1, views):
        tap_copy(shift).start()

    def rec_copy(shift, z):
        other, device = peer(shift)
        rows = pl.ds(pl.multiple_of(strip_of(other) * strip, strip), strip)
        return copy(
            flip_ref.at[z, rows],
            seen_ref.at[view, z],
            rec_send.at[shift - 1, z],
            rec_recv.at[view, z],
            device,
        )

    for z in range(depth):
        if z > 0:
            flip_ref[z] = rec_ref[0, 0, z].T
        for shift in range(1, views):
            rec_copy(shift, z).start()
        seen_ref[view, z] = flip_ref[z, pl.ds(first, strip)]

    for z in range(depth):
        wide_ref[z, EDGE : EDGE + broad] = init_ref[0, z].T

    def edge_west():
        return copy(
            wide_ref.at[:, EDGE : 2 * EDGE],
            wide_ref.at[:, EDGE + broad :],
            edge_send.at[0],
            edge_recv.at[0],
            {"tile": tile - 1, "view": view},
        )

    def edge_east():
        return copy(
            wide_ref.at[:, broad : EDGE + broad],
            wide_ref.at[:, 0:EDGE],
            edge_send.at[1],
            edge_recv.at[1],
            {"tile": tile + 1, "view": view},
        )

    @pl.when(tile > 0)
    def _():
        edge_west().start()

    @pl.when(tile < tiles - 1)
    def _():
        edge_east().start()

    @pl.when(tile == 0)
    def _():
        wide_ref[:, 0:EDGE] = jnp.zeros((depth, EDGE, tall), jnp.float32)

    @pl.when(tile == tiles - 1)
    def _():
        wide_ref[:, EDGE + broad :] = jnp.zeros((depth, EDGE, tall), jnp.float32)

    @pl.when(jnp.logical_not(has_west))
    def _():
        next_ref[:, 0:EDGE] = jnp.zeros((depth, EDGE, tall), jnp.float32)
        west_ref[...] = jnp.zeros(west_ref.shape, jnp.float32)

    @pl.when(jnp.logical_not(has_east))
    def _():
        next_ref[:, EDGE + strip :] = jnp.zeros((depth, EDGE, tall), jnp.float32)
        east_ref[...] = jnp.zeros(east_ref.shape, jnp.float32)

    def places(size, part, axis, shape):
        index = lax.broadcasted_iota(jnp.int32, shape, axis)
        plane = jnp.zeros(shape, jnp.int32)
        for z in range(1, depth):
            plane = plane + jnp.where(index >= z * part, 1, 0)
        return plane, index - plane * part

    def build(v, carry):
        @pl.when(v != view)
        def _():
            copy(
                taps_ref.at[v], taps_ref.at[v], tap_send.at[0], tap_recv.at[v], peer(1)[1]
            ).wait_recv()

        table = taps_ref[v]
        z_out, x_out = places(inner, strip, 0, (inner, outer))
        z_in, x_in = places(outer, span, 1, (inner, outer))
        along_x = x_in - x_out - (EDGE - HALF)
        along_z = z_in - z_out + HALF
        band = jnp.zeros((inner, outer), jnp.float32)
        for c in range(taps):
            band = jnp.where(along_x == c, table[0:1, c : c + 1], band)
        planes = jnp.zeros((inner, outer), jnp.float32)
        for c in range(max(0, HALF - depth + 1), min(taps, HALF + depth)):
            planes = jnp.where(along_z == c, table[2:3, c : c + 1], planes)
        both = band * planes
        g_hi[v], g_lo[v] = split(both)
        gt_hi[v], gt_lo[v] = split(both.T)
        shape = (tall, tall)
        along_y = lax.broadcasted_iota(jnp.int32, shape, 1) - lax.broadcasted_iota(
            jnp.int32, shape, 0
        )
        rows = jnp.zeros(shape, jnp.float32)
        for c in range(taps):
            rows = jnp.where(along_y + HALF == c, table[1:2, c : c + 1], rows)
        m_hi[v], m_lo[v] = split(rows)
        return carry

    lax.fori_loop(0, views, build, 0)

    def over_west(it, v):
        return copy(
            corr_ref.at[it, v, :, 0:EDGE],
            east_ref.at[it, v],
            over_send.at[it, 0, v],
            over_recv.at[it, 0, v],
            west_id,
        )

    def over_east(it, v):
        return copy(
            corr_ref.at[it, v, :, EDGE + strip :],
            west_ref.at[it, v],
            over_send.at[it, 1, v],
            over_recv.at[it, 1, v],
            east_id,
        )

    def halo_west():
        return copy(
            next_ref.at[:, EDGE : 2 * EDGE],
            next_ref.at[:, EDGE + strip :],
            halo_send.at[0],
            halo_recv.at[0],
            west_id,
        )

    def halo_east():
        return copy(
            next_ref.at[:, strip : EDGE + strip],
            next_ref.at[:, 0:EDGE],
            halo_send.at[1],
            halo_recv.at[1],
            east_id,
        )

    def forward(v):
        w = product((g_hi[v], g_lo[v]), (p_hi[...], p_lo[...]), (1, 0))
        return product(split(w), (m_hi[v], m_lo[v]), (1, 1))

    def back(it, v, blurred):
        ratio = seen_ref[v].reshape(inner, tall) / blurred
        a = product(split(ratio), (m_hi[v], m_lo[v]), (1, 0))
        c = product((gt_hi[v], gt_lo[v]), split(a), (1, 0))
        corr_ref[it, v] = c.reshape(depth, span, tall)

        @pl.when(has_west)
        def _():
            over_west(it, v).start()

        @pl.when(has_east)
        def _():
            over_east(it, v).start()

    def summed(it):
        def body(v, total):
            @pl.when(has_east)
            def _():
                over_west(it, v).wait_recv()

            @pl.when(has_west)
            def _():
                over_east(it, v).wait_recv()

            mid = corr_ref[it, v, :, EDGE : EDGE + strip]
            low = mid[:, :EDGE] + west_ref[it, v]
            high = mid[:, strip - EDGE :] + east_ref[it, v]
            full = jnp.concatenate([low, mid[:, EDGE : strip - EDGE], high], axis=1)
            return total + jnp.log(full)

        return lax.fori_loop(0, views, body, jnp.zeros((depth, strip, tall), jnp.float32))

    @pl.when(tile < tiles - 1)
    def _():
        edge_west().wait_recv()

    @pl.when(tile > 0)
    def _():
        edge_east().wait_recv()

    p_hi[...], p_lo[...] = split(wide_ref[:, pl.ds(first, span)].reshape(outer, tall))

    def ahead(v, carry):
        blur_ref[v] = forward(v)
        return carry

    lax.fori_loop(0, views, ahead, 0)

    def first_back(v, carry):
        @pl.when(v != view)
        def _():
            for z in range(depth):
                copy(
                    flip_ref.at[z, pl.ds(0, strip)],
                    seen_ref.at[v, z],
                    rec_send.at[0, z],
                    rec_recv.at[v, z],
                    peer(1)[1],
                ).wait_recv()

        back(0, v, blur_ref[v])
        return carry

    lax.fori_loop(0, views, first_back, 0)
    old = wide_ref[:, pl.ds(pl.multiple_of(first + EDGE, EDGE), strip)]
    new = old * jnp.exp(summed(0) / views)
    next_ref[:, EDGE : EDGE + strip] = new

    @pl.when(has_west)
    def _():
        halo_west().start()

    @pl.when(has_east)
    def _():
        halo_east().start()

    @pl.when(has_east)
    def _():
        halo_west().wait_recv()

    @pl.when(has_west)
    def _():
        halo_east().wait_recv()

    p_hi[...], p_lo[...] = split(next_ref[...].reshape(outer, tall))

    def second(v, carry):
        back(1, v, forward(v))
        return carry

    lax.fori_loop(0, views, second, 0)
    old = next_ref[:, EDGE : EDGE + strip]
    out_ref[0, :, pl.ds(first, strip)] = old * jnp.exp(summed(1) / views)

    def out_copy(shift):
        rows = pl.ds(first, strip)
        return copy(
            out_ref.at[0, :, rows],
            out_ref.at[0, :, rows],
            out_send.at[shift - 1],
            out_recv.at[view],
            peer(shift)[1],
        )

    for shift in range(1, views):
        out_copy(shift).start()
    for shift in range(1, views):
        other = peer(shift)[0]
        rows = pl.ds(pl.multiple_of(strip_of(other) * strip, strip), strip)
        copy(
            out_ref.at[0, :, rows],
            out_ref.at[0, :, rows],
            out_send.at[shift - 1],
            out_recv.at[other],
            peer(shift)[1],
        ).wait_recv()

    for shift in range(1, views):
        tap_copy(shift).wait_send()
        out_copy(shift).wait_send()
        for z in range(depth):
            rec_copy(shift, z).wait_send()

    @pl.when(tile > 0)
    def _():
        edge_west().wait_send()

    @pl.when(tile < tiles - 1)
    def _():
        edge_east().wait_send()

    @pl.when(has_west)
    def _():
        halo_west().wait_send()
        for it in range(ITERS):
            for v in range(views):
                over_west(it, v).wait_send()

    @pl.when(has_east)
    def _():
        halo_east().wait_send()
        for it in range(ITERS):
            for v in range(views):
                over_east(it, v).wait_send()


def by_strips(initial, recorded, tap_table, variants):
    views = lax.axis_size("view")
    depth, tall, broad = initial.shape[1:]
    strip = broad // views
    span = strip + 2 * EDGE
    inner, outer = depth * strip, depth * span
    f32, bf16 = jnp.float32, jnp.bfloat16
    vmem = pl.BlockSpec(memory_space=pltpu.VMEM)
    dma = pltpu.SemaphoreType.DMA
    flipped = pl.pallas_call(
        strips_kernel,
        out_shape=jax.ShapeDtypeStruct((1, depth, broad, tall), f32),
        in_specs=[vmem, vmem, vmem, pl.BlockSpec(memory_space=pltpu.SMEM)],
        out_specs=vmem,
        scratch_shapes=[
            pltpu.VMEM((depth, broad + 2 * EDGE, tall), f32),
            pltpu.VMEM((depth, broad, tall), f32),
            pltpu.VMEM((views, depth, strip, tall), f32),
            pltpu.VMEM((views, 8, 128), f32),
            pltpu.VMEM((views, inner, outer), bf16),
            pltpu.VMEM((views, inner, outer), bf16),
            pltpu.VMEM((views, outer, inner), bf16),
            pltpu.VMEM((views, outer, inner), bf16),
            pltpu.VMEM((views, tall, tall), bf16),
            pltpu.VMEM((views, tall, tall), bf16),
            pltpu.VMEM((outer, tall), bf16),
            pltpu.VMEM((outer, tall), bf16),
            pltpu.VMEM((views, inner, tall), f32),
            pltpu.VMEM((ITERS, views, depth, span, tall), f32),
            pltpu.VMEM((ITERS, views, depth, EDGE, tall), f32),
            pltpu.VMEM((ITERS, views, depth, EDGE, tall), f32),
            pltpu.VMEM((depth, span, tall), f32),
            dma((views - 1,)),
            dma((views,)),
            dma((views - 1, depth)),
            dma((views, depth)),
            dma((2,)),
            dma((2,)),
            dma((ITERS, 2, views)),
            dma((ITERS, 2, views)),
            dma((2,)),
            dma((2,)),
            dma((views - 1,)),
            dma((views,)),
        ],
        compiler_params=pltpu.CompilerParams(
            collective_id=0, has_side_effects=True, vmem_limit_bytes=40 * 2**20
        ),
        name="strips",
    )(initial, recorded, tap_table, variants)
    return jnp.swapaxes(flipped, 2, 3)


def solution(mesh):
    rows_of_tiles = mesh.shape["tile"] // GX
    return jax.shard_map(
        by_strips if rows_of_tiles == 1 else per_device,
        mesh=mesh,
        in_specs=(
            P("tile", None, None, None),
            P("view", "tile", None, None, None),
            P("view", None, None, None),
            P("view", None),
        ),
        out_specs=P("tile", None, None, None),
        check_vma=False,
    )
```

```python
import jax
import jax.numpy as jnp
from jax import lax
from jax.experimental import pallas as pl
from jax.experimental.pallas import tpu as pltpu
from jax.sharding import PartitionSpec as P

GX = 8
ITERS = 2
HALF = 15
EDGE = 16
MESH = pl.DeviceIdType.MESH


def passed_along(block, axis, distance):
    devices = range(lax.axis_size(axis))
    route = [(i - distance, i) for i in devices if i - distance in devices]
    return lax.ppermute(block, axis, route)


def normalized(tap_table):
    return tap_table / jnp.sum(tap_table, axis=-1, keepdims=True)


def tile_kernels(kernels, variant_ids, grid_rows, grid_cols):
    count_variants = kernels.shape[0]
    onehot = (variant_ids[:, None] == jnp.arange(count_variants, dtype=jnp.int32)[None, :]).astype(
        jnp.float32
    )
    flat = jnp.dot(onehot, kernels.reshape(count_variants, -1), precision=lax.Precision.HIGHEST)
    return flat.reshape(grid_rows, grid_cols, 3, kernels.shape[-1])


def tile_onehot(positions, extent, count):
    owner = jnp.clip(jnp.floor_divide(positions, extent), 0, count - 1)
    return (owner[:, None] == jnp.arange(count, dtype=jnp.int32)[None, :]).astype(jnp.float32)


def weight_map(tile_taps, axis_id, offset, row_hot, col_hot):
    inner = jnp.dot(row_hot, tile_taps[:, :, axis_id, offset], precision=lax.Precision.HIGHEST)
    return jnp.dot(inner, col_hot.T, precision=lax.Precision.HIGHEST)


def blur_cols(padded, tile_taps, row_hot, col_hot):
    count = col_hot.shape[0]
    result = jnp.zeros((padded.shape[0], padded.shape[1], count), jnp.float32)
    for offset in range(tile_taps.shape[3]):
        weights = weight_map(tile_taps, 0, offset, row_hot, col_hot)
        result = result + weights[None] * padded[:, :, offset : offset + count]
    return result


def blur_rows(padded, tile_taps, row_hot, col_hot):
    count = row_hot.shape[0]
    result = jnp.zeros((padded.shape[0], count, padded.shape[2]), jnp.float32)
    for offset in range(tile_taps.shape[3]):
        weights = weight_map(tile_taps, 1, offset, row_hot, col_hot)
        result = result + weights[None] * padded[:, offset : offset + count, :]
    return result


def blur_planes(field, tile_taps, row_hot, col_hot, reverse):
    taps = tile_taps.shape[3]
    margin = taps // 2
    padded = jnp.pad(field, ((margin, margin), (0, 0), (0, 0)))
    planes = field.shape[0]
    result = jnp.zeros(field.shape, jnp.float32)
    for offset in range(taps):
        which = taps - 1 - offset if reverse else offset
        weights = weight_map(tile_taps, 2, which, row_hot, col_hot)
        result = result + weights[None] * padded[offset : offset + planes]
    return result


def adjoint_rows(padded, tile_taps, row_hot, col_hot):
    margin = tile_taps.shape[3] // 2
    count = padded.shape[1] - 2 * margin
    result = jnp.zeros((padded.shape[0], count, padded.shape[2]), jnp.float32)
    for offset in range(tile_taps.shape[3]):
        lead = 2 * margin - offset
        weights = weight_map(tile_taps, 1, offset, row_hot, col_hot)
        result = result + weights[None, lead : lead + count, :] * padded[:, lead : lead + count, :]
    return result


def adjoint_cols(padded, tile_taps, row_hot, col_hot):
    margin = tile_taps.shape[3] // 2
    count = padded.shape[2] - 2 * margin
    result = jnp.zeros((padded.shape[0], padded.shape[1], count), jnp.float32)
    for offset in range(tile_taps.shape[3]):
        lead = 2 * margin - offset
        weights = weight_map(tile_taps, 0, offset, row_hot, col_hot)
        result = result + weights[None, :, lead : lead + count] * padded[:, :, lead : lead + count]
    return result


def widen_cols(field, width, tile_col):
    west_send = field[:, :, -width:]
    east_send = field[:, :, :width]
    west_send = jnp.where(tile_col < GX - 1, west_send, jnp.zeros_like(west_send))
    east_send = jnp.where(tile_col > 0, east_send, jnp.zeros_like(east_send))
    from_west = passed_along(west_send, "tile", 1)
    from_east = passed_along(east_send, "tile", -1)
    return jnp.concatenate([from_west, field, from_east], axis=2)


def widen_rows(field, width):
    from_north = passed_along(field[:, -width:, :], "tile", GX)
    from_south = passed_along(field[:, :width, :], "tile", -GX)
    return jnp.concatenate([from_north, field, from_south], axis=1)


def per_device(initial, recorded, tap_table, variants):
    position = lax.axis_index("tile")
    count_tiles = lax.axis_size("tile")
    count_views = lax.axis_size("view")
    grid_rows = count_tiles // GX
    tile_row = position // GX
    tile_col = position % GX
    tile_taps = tile_kernels(normalized(tap_table[0]), variants[0], grid_rows, GX)
    estimate = initial[0]
    observed = recorded[0, 0]
    tall = estimate.shape[1]
    broad = estimate.shape[2]
    row_first = tile_row * tall
    col_first = tile_col * broad

    def row_places(margin):
        return row_first + jnp.arange(tall + 2 * margin, dtype=jnp.int32) - margin

    def col_places(margin):
        return col_first + jnp.arange(broad + 2 * margin, dtype=jnp.int32) - margin

    own_rows = tile_onehot(row_places(0), tall, grid_rows)
    own_cols = tile_onehot(col_places(0), broad, GX)
    wide_rows = tile_onehot(row_places(HALF), tall, grid_rows)
    wide_cols = tile_onehot(col_places(HALF), broad, GX)
    for step in range(ITERS):
        padded = widen_cols(estimate, HALF, tile_col)
        planes = blur_planes(
            blur_cols(padded, tile_taps, own_rows, own_cols), tile_taps, own_rows, own_cols, False
        )
        blurred = blur_rows(widen_rows(planes, HALF), tile_taps, own_rows, own_cols)
        ratio = observed / blurred
        back = adjoint_rows(widen_rows(ratio, HALF), tile_taps, wide_rows, own_cols)
        back = blur_planes(back, tile_taps, own_rows, own_cols, True)
        correction = adjoint_cols(widen_cols(back, HALF, tile_col), tile_taps, own_rows, wide_cols)
        logged = jnp.log(correction)
        summed = lax.psum(logged, "view")
        estimate = estimate * jnp.exp(summed / count_views)
    return estimate[None]


def split(value):
    high = value.astype(jnp.bfloat16)
    return high, (value - high.astype(jnp.float32)).astype(jnp.bfloat16)


def product(left, right, contract):
    dims = (((contract[0],), (contract[1],)), ((), ()))

    def one(a, b):
        return lax.dot_general(a, b, dims, preferred_element_type=jnp.float32)

    return one(left[0], right[0]) + (one(left[0], right[1]) + one(left[1], right[0]))


def strips_kernel(
    init_hbm,
    rec_hbm,
    tap_hbm,
    var_ref,
    out_ref,
    init_ref,
    rec_ref,
    tap_ref,
    wide_ref,
    flip_ref,
    seen_ref,
    taps_ref,
    g_hi,
    g_lo,
    gt_hi,
    gt_lo,
    m_hi,
    m_lo,
    p_hi,
    p_lo,
    a_hi,
    a_lo,
    blur_ref,
    corr_ref,
    west_ref,
    east_ref,
    next_ref,
    load_sem,
    tap_send,
    tap_recv,
    rec_send,
    rec_recv,
    edge_send,
    edge_recv,
    over_send,
    over_recv,
    halo_send,
    halo_recv,
    out_send,
    out_recv,
):
    tile = lax.axis_index("tile")
    view = lax.axis_index("view")
    tiles = lax.axis_size("tile")
    views = lax.axis_size("view")
    depth, tall, broad = init_ref.shape
    strip = broad // views
    span = strip + 2 * EDGE
    inner, outer = depth * strip, depth * span
    taps = tap_ref.shape[2]
    parts = (1, 2)

    tap_load = pltpu.make_async_copy(tap_hbm.at[0], tap_ref, load_sem.at[0])
    init_load = pltpu.make_async_copy(init_hbm.at[0], init_ref, load_sem.at[1])
    rec_loads = [
        pltpu.make_async_copy(rec_hbm.at[0, 0, z], rec_ref.at[z], load_sem.at[2 + z])
        for z in range(depth)
    ]
    tap_load.start()
    for z in range(depth):
        rec_loads[z].start()
    init_load.start()

    def strip_of(position):
        odd = lax.rem(tile, 2)
        return position + odd * (views - 1 - 2 * position)

    mine = strip_of(view)
    has_west = (tile > 0) | (mine > 0)
    has_east = (tile < tiles - 1) | (mine < views - 1)
    step = 1 - 2 * lax.rem(tile, 2)
    west_id = {
        "tile": jnp.where(mine > 0, tile, tile - 1),
        "view": jnp.where(mine > 0, view - step, view),
    }
    east_id = {
        "tile": jnp.where(mine < views - 1, tile, tile + 1),
        "view": jnp.where(mine < views - 1, view + step, view),
    }
    first = pl.multiple_of(mine * strip, strip)

    half = views // 2
    side, place = view // half, lax.rem(view, half)

    def peer(order):
        if order < half:
            other = (1 - side) * half + lax.rem(place + order, half)
        else:
            other = side * half + lax.rem(place + order - half + 1, half)
        return other, {"tile": tile, "view": other}

    def copy(source, target, send, recv, device):
        return pltpu.make_async_remote_copy(
            src_ref=source,
            dst_ref=target,
            send_sem=send,
            recv_sem=recv,
            device_id=device,
            device_id_type=MESH,
        )

    barrier = pltpu.get_barrier_semaphore()
    for shift in range(views - 1):
        pl.semaphore_signal(barrier, inc=1, device_id=peer(shift)[1], device_id_type=MESH)

    @pl.when(tile > 0)
    def _():
        pl.semaphore_signal(
            barrier, inc=1, device_id={"tile": tile - 1, "view": view}, device_id_type=MESH
        )

    @pl.when(tile < tiles - 1)
    def _():
        pl.semaphore_signal(
            barrier, inc=1, device_id={"tile": tile + 1, "view": view}, device_id_type=MESH
        )

    tap_load.wait()
    chosen = lax.broadcasted_iota(jnp.int32, tap_ref.shape[1:], 0) == var_ref[0, tile]
    taps_ref[view] = jnp.zeros(taps_ref.shape[1:], jnp.float32)
    for a in range(tap_ref.shape[0]):
        own_taps = jnp.sum(jnp.where(chosen, tap_ref[a], 0.0), axis=0, keepdims=True)
        own_taps = own_taps / jnp.sum(own_taps, axis=-1, keepdims=True)
        taps_ref[view, a : a + 1, 0:taps] = own_taps
    rec_loads[0].wait()
    flip_ref[0] = rec_ref[0].T

    pl.semaphore_wait(
        barrier, views - 1 + jnp.where(tile > 0, 1, 0) + jnp.where(tile < tiles - 1, 1, 0)
    )

    def tap_copy(shift):
        return copy(
            taps_ref.at[view],
            taps_ref.at[view],
            tap_send.at[shift],
            tap_recv.at[view],
            peer(shift)[1],
        )

    for shift in range(views - 1):
        tap_copy(shift).start()

    def rec_copy(shift, z):
        other, device = peer(shift)
        rows = pl.ds(pl.multiple_of(strip_of(other) * strip, strip), strip)
        return copy(
            flip_ref.at[z, rows],
            seen_ref.at[view, z],
            rec_send.at[shift, z],
            rec_recv.at[view, z],
            device,
        )

    for z in range(depth):
        if z > 0:
            rec_loads[z].wait()
            flip_ref[z] = rec_ref[z].T
        rec_copy(0, z).start()
        seen_ref[view, z] = flip_ref[z, pl.ds(first, strip)]

    for shift in range(1, views - 1):
        for z in range(depth):
            rec_copy(shift, z).start()

    init_load.wait()
    for z in range(depth):
        wide_ref[z, EDGE : EDGE + broad] = init_ref[z].T

    def edge_west():
        return copy(
            wide_ref.at[:, EDGE : 2 * EDGE],
            wide_ref.at[:, EDGE + broad :],
            edge_send.at[0],
            edge_recv.at[0],
            {"tile": tile - 1, "view": view},
        )

    def edge_east():
        return copy(
            wide_ref.at[:, broad : EDGE + broad],
            wide_ref.at[:, 0:EDGE],
            edge_send.at[1],
            edge_recv.at[1],
            {"tile": tile + 1, "view": view},
        )

    @pl.when(tile > 0)
    def _():
        edge_west().start()

    @pl.when(tile < tiles - 1)
    def _():
        edge_east().start()

    @pl.when(tile == 0)
    def _():
        wide_ref[:, 0:EDGE] = jnp.zeros((depth, EDGE, tall), jnp.float32)

    @pl.when(tile == tiles - 1)
    def _():
        wide_ref[:, EDGE + broad :] = jnp.zeros((depth, EDGE, tall), jnp.float32)

    @pl.when(jnp.logical_not(has_west))
    def _():
        next_ref[:, 0:EDGE] = jnp.zeros((depth, EDGE, tall), jnp.float32)
        west_ref[...] = jnp.zeros(west_ref.shape, jnp.float32)

    @pl.when(jnp.logical_not(has_east))
    def _():
        next_ref[:, EDGE + strip :] = jnp.zeros((depth, EDGE, tall), jnp.float32)
        east_ref[...] = jnp.zeros(east_ref.shape, jnp.float32)

    def places(size, part, axis, shape):
        index = lax.broadcasted_iota(jnp.int32, shape, axis)
        plane = jnp.zeros(shape, jnp.int32)
        for z in range(1, depth):
            plane = plane + jnp.where(index >= z * part, 1, 0)
        return plane, index - plane * part

    def build(v, carry):
        @pl.when(v != view)
        def _():
            copy(
                taps_ref.at[v], taps_ref.at[v], tap_send.at[0], tap_recv.at[v], peer(1)[1]
            ).wait_recv()

        table = taps_ref[v]
        z_out, x_out = places(inner, strip, 0, (inner, outer))
        z_in, x_in = places(outer, span, 1, (inner, outer))
        along_x = x_in - x_out - (EDGE - HALF)
        along_z = z_in - z_out + HALF
        band = jnp.zeros((inner, outer), jnp.float32)
        for c in range(taps):
            band = jnp.where(along_x == c, table[0:1, c : c + 1], band)
        planes = jnp.zeros((inner, outer), jnp.float32)
        for c in range(max(0, HALF - depth + 1), min(taps, HALF + depth)):
            planes = jnp.where(along_z == c, table[2:3, c : c + 1], planes)
        both = band * planes
        g_hi[v], g_lo[v] = split(both)
        gt_hi[v], gt_lo[v] = split(both.T)
        shape = (tall, tall)
        along_y = lax.broadcasted_iota(jnp.int32, shape, 1) - lax.broadcasted_iota(
            jnp.int32, shape, 0
        )
        rows = jnp.zeros(shape, jnp.float32)
        for c in range(taps):
            rows = jnp.where(along_y + HALF == c, table[1:2, c : c + 1], rows)
        m_hi[v], m_lo[v] = split(rows)
        return carry

    lax.fori_loop(0, views, build, 0)

    def over_west(it, v, part):
        planes = pl.ds(part * (depth // parts[it]), depth // parts[it])
        return copy(
            corr_ref.at[it, v, planes, 0:EDGE],
            east_ref.at[it, v, planes],
            over_send.at[it, 0, v, part],
            over_recv.at[it, 0, v, part],
            west_id,
        )

    def over_east(it, v, part):
        planes = pl.ds(part * (depth // parts[it]), depth // parts[it])
        return copy(
            corr_ref.at[it, v, planes, EDGE + strip :],
            west_ref.at[it, v, planes],
            over_send.at[it, 1, v, part],
            over_recv.at[it, 1, v, part],
            east_id,
        )

    def send_over(it, v, part):
        @pl.when(has_west)
        def _():
            over_west(it, v, part).start()

        @pl.when(has_east)
        def _():
            over_east(it, v, part).start()

    def halo_west():
        return copy(
            next_ref.at[:, EDGE : 2 * EDGE],
            next_ref.at[:, EDGE + strip :],
            halo_send.at[0],
            halo_recv.at[0],
            west_id,
        )

    def halo_east():
        return copy(
            next_ref.at[:, strip : EDGE + strip],
            next_ref.at[:, 0:EDGE],
            halo_send.at[1],
            halo_recv.at[1],
            east_id,
        )

    def forward(*vs):
        spread = [product((g_hi[v], g_lo[v]), (p_hi[...], p_lo[...]), (1, 0)) for v in vs]
        return [
            product(split(w), (m_hi[v], m_lo[v]), (1, 1)) for v, w in zip(vs, spread)
        ]

    def gathered(v, blurred):
        ratio = seen_ref[v].reshape(inner, tall) / blurred
        return split(product(split(ratio), (m_hi[v], m_lo[v]), (1, 0)))

    def arrived(it, part):
        def body(v, carry):
            @pl.when(has_east)
            def _():
                over_west(it, v, part).wait_recv()

            @pl.when(has_west)
            def _():
                over_east(it, v, part).wait_recv()

            return carry

        lax.fori_loop(0, views, body, 0)

    def factor(it, z):
        total = jnp.zeros((strip, tall), jnp.float32)
        for v in range(views):
            mid = corr_ref[it, v, z, EDGE : EDGE + strip]
            low = mid[:EDGE] + west_ref[it, v, z]
            high = mid[strip - EDGE :] + east_ref[it, v, z]
            total = total + jnp.log(
                jnp.concatenate([low, mid[EDGE : strip - EDGE], high], axis=0)
            )
        return jnp.exp(total / views)

    @pl.when(tile < tiles - 1)
    def _():
        edge_west().wait_recv()

    @pl.when(tile > 0)
    def _():
        edge_east().wait_recv()

    p_hi[...], p_lo[...] = split(wide_ref[:, pl.ds(first, span)].reshape(outer, tall))

    def ahead(i, carry):
        blur_ref[2 * i], blur_ref[2 * i + 1] = forward(2 * i, 2 * i + 1)
        return carry

    lax.fori_loop(0, views // 2, ahead, 0)

    def first_back(k, carry):
        from_side = jnp.where(k < half, side, 1 - side)
        v = from_side * half + lax.rem(place + k, half)

        @pl.when(v != view)
        def _():
            for z in range(depth):
                copy(
                    flip_ref.at[z, pl.ds(0, strip)],
                    seen_ref.at[v, z],
                    rec_send.at[0, z],
                    rec_recv.at[v, z],
                    peer(1)[1],
                ).wait_recv()

        a = gathered(v, blur_ref[v])
        corr_ref[0, v] = product((gt_hi[v], gt_lo[v]), a, (1, 0)).reshape(depth, span, tall)
        send_over(0, v, 0)
        return carry

    lax.fori_loop(0, views, first_back, 0)
    arrived(0, 0)
    for z in range(depth):
        old = wide_ref[z, pl.ds(pl.multiple_of(first + EDGE, EDGE), strip)]
        next_ref[z, EDGE : EDGE + strip] = old * factor(0, z)

    @pl.when(has_west)
    def _():
        halo_west().start()

    @pl.when(has_east)
    def _():
        halo_east().start()

    @pl.when(has_east)
    def _():
        halo_west().wait_recv()

    @pl.when(has_west)
    def _():
        halo_east().wait_recv()

    p_hi[...], p_lo[...] = split(next_ref[...].reshape(outer, tall))

    planes = depth // parts[1]

    def spread_back(part, *vs):
        rows = slice(part * planes * span, (part + 1) * planes * span)
        for v in vs:
            c = product((gt_hi[v, rows], gt_lo[v, rows]), (a_hi[v], a_lo[v]), (1, 0))
            corr_ref[1, v, part * planes : (part + 1) * planes] = c.reshape(planes, span, tall)
        for v in vs:
            send_over(1, v, part)

    def second(i, carry):
        vs = 2 * i, 2 * i + 1
        for v, blurred in zip(vs, forward(*vs)):
            a_hi[v], a_lo[v] = gathered(v, blurred)
        spread_back(0, *vs)
        return carry

    lax.fori_loop(0, views // 2, second, 0)

    def rest(i, carry):
        spread_back(1, 2 * i, 2 * i + 1)
        return carry

    lax.fori_loop(0, views // 2, rest, 0)

    def out_copy(source, z, way):
        rows = out_ref.at[
            0, z, pl.ds(pl.multiple_of(strip_of(source) * strip, strip), strip)
        ]
        return copy(
            rows,
            rows,
            out_send.at[way, source, z],
            out_recv.at[source, z],
            {"tile": tile, "view": view + 2 * way - 1},
        )

    for z in range(depth):
        if z % planes == 0:
            arrived(1, z // planes)
        out_ref[0, z, pl.ds(first, strip)] = next_ref[z, EDGE : EDGE + strip] * factor(1, z)

        @pl.when(view < views - 1)
        def _():
            out_copy(view, z, 1).start()

        @pl.when(view > 0)
        def _():
            out_copy(view, z, 0).start()

    for distance in range(1, views):
        for z in range(depth):

            @pl.when(view >= distance)
            def _():
                out_copy(view - distance, z, 1).wait_recv()

                @pl.when(view < views - 1)
                def _():
                    out_copy(view - distance, z, 1).start()

            @pl.when(view + distance < views)
            def _():
                out_copy(view + distance, z, 0).wait_recv()

                @pl.when(view > 0)
                def _():
                    out_copy(view + distance, z, 0).start()

    for shift in range(views - 1):
        tap_copy(shift).wait_send()
        for z in range(depth):
            rec_copy(shift, z).wait_send()

    for source in range(views):

        @pl.when((source <= view) & (view < views - 1))
        def _():
            for z in range(depth):
                out_copy(source, z, 1).wait_send()

        @pl.when((source >= view) & (view > 0))
        def _():
            for z in range(depth):
                out_copy(source, z, 0).wait_send()

    @pl.when(tile > 0)
    def _():
        edge_west().wait_send()

    @pl.when(tile < tiles - 1)
    def _():
        edge_east().wait_send()

    @pl.when(has_west)
    def _():
        halo_west().wait_send()
        for it in range(ITERS):
            for v in range(views):
                for part in range(parts[it]):
                    over_west(it, v, part).wait_send()

    @pl.when(has_east)
    def _():
        halo_east().wait_send()
        for it in range(ITERS):
            for v in range(views):
                for part in range(parts[it]):
                    over_east(it, v, part).wait_send()


def by_strips(initial, recorded, tap_table, variants):
    views = lax.axis_size("view")
    depth, tall, broad = initial.shape[1:]
    strip = broad // views
    span = strip + 2 * EDGE
    inner, outer = depth * strip, depth * span
    f32, bf16 = jnp.float32, jnp.bfloat16
    vmem = pl.BlockSpec(memory_space=pltpu.VMEM)
    anywhere = pl.BlockSpec(memory_space=pl.ANY)
    dma = pltpu.SemaphoreType.DMA
    by_axis = jnp.swapaxes(tap_table, 1, 2)
    flipped = pl.pallas_call(
        strips_kernel,
        out_shape=jax.ShapeDtypeStruct((1, depth, broad, tall), f32),
        in_specs=[anywhere, anywhere, anywhere, pl.BlockSpec(memory_space=pltpu.SMEM)],
        out_specs=vmem,
        scratch_shapes=[
            pltpu.VMEM((depth, tall, broad), f32),
            pltpu.VMEM((depth, tall, broad), f32),
            pltpu.VMEM(by_axis.shape[1:], f32),
            pltpu.VMEM((depth, broad + 2 * EDGE, tall), f32),
            pltpu.VMEM((depth, broad, tall), f32),
            pltpu.VMEM((views, depth, strip, tall), f32),
            pltpu.VMEM((views, 8, 128), f32),
            pltpu.VMEM((views, inner, outer), bf16),
            pltpu.VMEM((views, inner, outer), bf16),
            pltpu.VMEM((views, outer, inner), bf16),
            pltpu.VMEM((views, outer, inner), bf16),
            pltpu.VMEM((views, tall, tall), bf16),
            pltpu.VMEM((views, tall, tall), bf16),
            pltpu.VMEM((outer, tall), bf16),
            pltpu.VMEM((outer, tall), bf16),
            pltpu.VMEM((views, inner, tall), bf16),
            pltpu.VMEM((views, inner, tall), bf16),
            pltpu.VMEM((views, inner, tall), f32),
            pltpu.VMEM((ITERS, views, depth, span, tall), f32),
            pltpu.VMEM((ITERS, views, depth, EDGE, tall), f32),
            pltpu.VMEM((ITERS, views, depth, EDGE, tall), f32),
            pltpu.VMEM((depth, span, tall), f32),
            dma((2 + depth,)),
            dma((views - 1,)),
            dma((views,)),
            dma((views - 1, depth)),
            dma((views, depth)),
            dma((2,)),
            dma((2,)),
            dma((ITERS, 2, views, 2)),
            dma((ITERS, 2, views, 2)),
            dma((2,)),
            dma((2,)),
            dma((2, views, depth)),
            dma((views, depth)),
        ],
        compiler_params=pltpu.CompilerParams(
            collective_id=0, has_side_effects=True, vmem_limit_bytes=56 * 2**20
        ),
        name="strips",
    )(initial, recorded, by_axis, variants)
    return jnp.swapaxes(flipped, 2, 3)


def solution(mesh):
    rows_of_tiles = mesh.shape["tile"] // GX
    return jax.shard_map(
        by_strips if rows_of_tiles == 1 else per_device,
        mesh=mesh,
        in_specs=(
            P("tile", None, None, None),
            P("view", "tile", None, None, None),
            P("view", None, None, None),
            P("view", None),
        ),
        out_specs=P("tile", None, None, None),
        check_vma=False,
    )
```

```python
import jax
import jax.numpy as jnp
from jax import lax
from jax.experimental import pallas as pl
from jax.experimental.pallas import tpu as pltpu
from jax.sharding import PartitionSpec as P

GX = 8
ITERS = 2
HALF = 15
EDGE = 16
MESH = pl.DeviceIdType.MESH


def passed_along(block, axis, distance):
    devices = range(lax.axis_size(axis))
    route = [(i - distance, i) for i in devices if i - distance in devices]
    return lax.ppermute(block, axis, route)


def normalized(tap_table):
    return tap_table / jnp.sum(tap_table, axis=-1, keepdims=True)


def tile_kernels(kernels, variant_ids, grid_rows, grid_cols):
    count_variants = kernels.shape[0]
    onehot = (variant_ids[:, None] == jnp.arange(count_variants, dtype=jnp.int32)[None, :]).astype(
        jnp.float32
    )
    flat = jnp.dot(onehot, kernels.reshape(count_variants, -1), precision=lax.Precision.HIGHEST)
    return flat.reshape(grid_rows, grid_cols, 3, kernels.shape[-1])


def tile_onehot(positions, extent, count):
    owner = jnp.clip(jnp.floor_divide(positions, extent), 0, count - 1)
    return (owner[:, None] == jnp.arange(count, dtype=jnp.int32)[None, :]).astype(jnp.float32)


def weight_map(tile_taps, axis_id, offset, row_hot, col_hot):
    inner = jnp.dot(row_hot, tile_taps[:, :, axis_id, offset], precision=lax.Precision.HIGHEST)
    return jnp.dot(inner, col_hot.T, precision=lax.Precision.HIGHEST)


def blur_cols(padded, tile_taps, row_hot, col_hot):
    count = col_hot.shape[0]
    result = jnp.zeros((padded.shape[0], padded.shape[1], count), jnp.float32)
    for offset in range(tile_taps.shape[3]):
        weights = weight_map(tile_taps, 0, offset, row_hot, col_hot)
        result = result + weights[None] * padded[:, :, offset : offset + count]
    return result


def blur_rows(padded, tile_taps, row_hot, col_hot):
    count = row_hot.shape[0]
    result = jnp.zeros((padded.shape[0], count, padded.shape[2]), jnp.float32)
    for offset in range(tile_taps.shape[3]):
        weights = weight_map(tile_taps, 1, offset, row_hot, col_hot)
        result = result + weights[None] * padded[:, offset : offset + count, :]
    return result


def blur_planes(field, tile_taps, row_hot, col_hot, reverse):
    taps = tile_taps.shape[3]
    margin = taps // 2
    padded = jnp.pad(field, ((margin, margin), (0, 0), (0, 0)))
    planes = field.shape[0]
    result = jnp.zeros(field.shape, jnp.float32)
    for offset in range(taps):
        which = taps - 1 - offset if reverse else offset
        weights = weight_map(tile_taps, 2, which, row_hot, col_hot)
        result = result + weights[None] * padded[offset : offset + planes]
    return result


def adjoint_rows(padded, tile_taps, row_hot, col_hot):
    margin = tile_taps.shape[3] // 2
    count = padded.shape[1] - 2 * margin
    result = jnp.zeros((padded.shape[0], count, padded.shape[2]), jnp.float32)
    for offset in range(tile_taps.shape[3]):
        lead = 2 * margin - offset
        weights = weight_map(tile_taps, 1, offset, row_hot, col_hot)
        result = result + weights[None, lead : lead + count, :] * padded[:, lead : lead + count, :]
    return result


def adjoint_cols(padded, tile_taps, row_hot, col_hot):
    margin = tile_taps.shape[3] // 2
    count = padded.shape[2] - 2 * margin
    result = jnp.zeros((padded.shape[0], padded.shape[1], count), jnp.float32)
    for offset in range(tile_taps.shape[3]):
        lead = 2 * margin - offset
        weights = weight_map(tile_taps, 0, offset, row_hot, col_hot)
        result = result + weights[None, :, lead : lead + count] * padded[:, :, lead : lead + count]
    return result


def widen_cols(field, width, tile_col):
    west_send = field[:, :, -width:]
    east_send = field[:, :, :width]
    west_send = jnp.where(tile_col < GX - 1, west_send, jnp.zeros_like(west_send))
    east_send = jnp.where(tile_col > 0, east_send, jnp.zeros_like(east_send))
    from_west = passed_along(west_send, "tile", 1)
    from_east = passed_along(east_send, "tile", -1)
    return jnp.concatenate([from_west, field, from_east], axis=2)


def widen_rows(field, width):
    from_north = passed_along(field[:, -width:, :], "tile", GX)
    from_south = passed_along(field[:, :width, :], "tile", -GX)
    return jnp.concatenate([from_north, field, from_south], axis=1)


def per_device(initial, recorded, tap_table, variants):
    position = lax.axis_index("tile")
    count_tiles = lax.axis_size("tile")
    count_views = lax.axis_size("view")
    grid_rows = count_tiles // GX
    tile_row = position // GX
    tile_col = position % GX
    tile_taps = tile_kernels(normalized(tap_table[0]), variants[0], grid_rows, GX)
    estimate = initial[0]
    observed = recorded[0, 0]
    tall = estimate.shape[1]
    broad = estimate.shape[2]
    row_first = tile_row * tall
    col_first = tile_col * broad

    def row_places(margin):
        return row_first + jnp.arange(tall + 2 * margin, dtype=jnp.int32) - margin

    def col_places(margin):
        return col_first + jnp.arange(broad + 2 * margin, dtype=jnp.int32) - margin

    own_rows = tile_onehot(row_places(0), tall, grid_rows)
    own_cols = tile_onehot(col_places(0), broad, GX)
    wide_rows = tile_onehot(row_places(HALF), tall, grid_rows)
    wide_cols = tile_onehot(col_places(HALF), broad, GX)
    for step in range(ITERS):
        padded = widen_cols(estimate, HALF, tile_col)
        planes = blur_planes(
            blur_cols(padded, tile_taps, own_rows, own_cols), tile_taps, own_rows, own_cols, False
        )
        blurred = blur_rows(widen_rows(planes, HALF), tile_taps, own_rows, own_cols)
        ratio = observed / blurred
        back = adjoint_rows(widen_rows(ratio, HALF), tile_taps, wide_rows, own_cols)
        back = blur_planes(back, tile_taps, own_rows, own_cols, True)
        correction = adjoint_cols(widen_cols(back, HALF, tile_col), tile_taps, own_rows, wide_cols)
        logged = jnp.log(correction)
        summed = lax.psum(logged, "view")
        estimate = estimate * jnp.exp(summed / count_views)
    return estimate[None]


def split(value):
    high = value.astype(jnp.bfloat16)
    return high, (value - high.astype(jnp.float32)).astype(jnp.bfloat16)


def product(left, right, contract):
    dims = (((contract[0],), (contract[1],)), ((), ()))

    def one(a, b):
        return lax.dot_general(a, b, dims, preferred_element_type=jnp.float32)

    return one(left[0], right[0]) + (one(left[0], right[1]) + one(left[1], right[0]))


def strips_kernel(
    init_hbm,
    rec_hbm,
    tap_hbm,
    var_ref,
    out_ref,
    init_ref,
    rec_ref,
    tap_ref,
    wide_ref,
    flip_ref,
    seen_ref,
    taps_ref,
    g_hi,
    g_lo,
    gt_hi,
    gt_lo,
    m_hi,
    m_lo,
    p_hi,
    p_lo,
    whole_ref,
    a_hi,
    a_lo,
    blur_ref,
    corr_ref,
    west_ref,
    east_ref,
    next_ref,
    load_sem,
    tap_send,
    tap_recv,
    rec_send,
    rec_recv,
    edge_send,
    edge_recv,
    over_send,
    over_recv,
    halo_send,
    halo_recv,
    out_send,
    out_recv,
):
    tile = lax.axis_index("tile")
    view = lax.axis_index("view")
    tiles = lax.axis_size("tile")
    views = lax.axis_size("view")
    depth, tall, broad = init_ref.shape
    strip = broad // views
    span = strip + 2 * EDGE
    inner, outer = depth * strip, depth * span
    taps = tap_ref.shape[2]
    parts = (1, 2)

    tap_load = pltpu.make_async_copy(tap_hbm.at[0], tap_ref, load_sem.at[0])
    init_load = pltpu.make_async_copy(init_hbm.at[0], init_ref, load_sem.at[1])
    rec_loads = [
        pltpu.make_async_copy(rec_hbm.at[0, 0, z], rec_ref.at[z], load_sem.at[2 + z])
        for z in range(depth)
    ]
    tap_load.start()
    for z in range(depth):
        rec_loads[z].start()
    init_load.start()

    def strip_of(position):
        odd = lax.rem(tile, 2)
        return position + odd * (views - 1 - 2 * position)

    mine = strip_of(view)
    has_west = (tile > 0) | (mine > 0)
    has_east = (tile < tiles - 1) | (mine < views - 1)
    step = 1 - 2 * lax.rem(tile, 2)
    west_id = {
        "tile": jnp.where(mine > 0, tile, tile - 1),
        "view": jnp.where(mine > 0, view - step, view),
    }
    east_id = {
        "tile": jnp.where(mine < views - 1, tile, tile + 1),
        "view": jnp.where(mine < views - 1, view + step, view),
    }
    first = pl.multiple_of(mine * strip, strip)

    half = views // 2
    side, place = view // half, lax.rem(view, half)

    def peer(order):
        if order < half:
            other = (1 - side) * half + lax.rem(place + order, half)
        else:
            other = side * half + lax.rem(place + order - half + 1, half)
        return other, {"tile": tile, "view": other}

    def copy(source, target, send, recv, device):
        return pltpu.make_async_remote_copy(
            src_ref=source,
            dst_ref=target,
            send_sem=send,
            recv_sem=recv,
            device_id=device,
            device_id_type=MESH,
        )

    barrier = pltpu.get_barrier_semaphore()
    for shift in range(views - 1):
        pl.semaphore_signal(barrier, inc=1, device_id=peer(shift)[1], device_id_type=MESH)

    @pl.when(tile > 0)
    def _():
        pl.semaphore_signal(
            barrier, inc=1, device_id={"tile": tile - 1, "view": view}, device_id_type=MESH
        )

    @pl.when(tile < tiles - 1)
    def _():
        pl.semaphore_signal(
            barrier, inc=1, device_id={"tile": tile + 1, "view": view}, device_id_type=MESH
        )

    tap_load.wait()
    chosen = lax.broadcasted_iota(jnp.int32, tap_ref.shape[1:], 0) == var_ref[0, tile]
    taps_ref[view] = jnp.zeros(taps_ref.shape[1:], jnp.float32)
    for a in range(tap_ref.shape[0]):
        own_taps = jnp.sum(jnp.where(chosen, tap_ref[a], 0.0), axis=0, keepdims=True)
        own_taps = own_taps / jnp.sum(own_taps, axis=-1, keepdims=True)
        taps_ref[view, a : a + 1, 0:taps] = own_taps
    rec_loads[0].wait()
    flip_ref[0] = rec_ref[0].T

    pl.semaphore_wait(
        barrier, views - 1 + jnp.where(tile > 0, 1, 0) + jnp.where(tile < tiles - 1, 1, 0)
    )

    def tap_copy(shift):
        return copy(
            taps_ref.at[view],
            taps_ref.at[view],
            tap_send.at[shift],
            tap_recv.at[view],
            peer(shift)[1],
        )

    for shift in range(views - 1):
        tap_copy(shift).start()

    def rec_copy(shift, z):
        other, device = peer(shift)
        rows = pl.ds(pl.multiple_of(strip_of(other) * strip, strip), strip)
        return copy(
            flip_ref.at[z, rows],
            seen_ref.at[view, z],
            rec_send.at[shift, z],
            rec_recv.at[view, z],
            device,
        )

    for z in range(depth):
        if z > 0:
            rec_loads[z].wait()
            flip_ref[z] = rec_ref[z].T
        rec_copy(0, z).start()
        seen_ref[view, z] = flip_ref[z, pl.ds(first, strip)]

    for shift in range(1, views - 1):
        for z in range(depth):
            rec_copy(shift, z).start()

    init_load.wait()
    for z in range(depth):
        wide_ref[z, EDGE : EDGE + broad] = init_ref[z].T

    def edge_west():
        return copy(
            wide_ref.at[:, EDGE : 2 * EDGE],
            wide_ref.at[:, EDGE + broad :],
            edge_send.at[0],
            edge_recv.at[0],
            {"tile": tile - 1, "view": view},
        )

    def edge_east():
        return copy(
            wide_ref.at[:, broad : EDGE + broad],
            wide_ref.at[:, 0:EDGE],
            edge_send.at[1],
            edge_recv.at[1],
            {"tile": tile + 1, "view": view},
        )

    @pl.when(tile > 0)
    def _():
        edge_west().start()

    @pl.when(tile < tiles - 1)
    def _():
        edge_east().start()

    @pl.when(tile == 0)
    def _():
        wide_ref[:, 0:EDGE] = jnp.zeros((depth, EDGE, tall), jnp.float32)

    @pl.when(tile == tiles - 1)
    def _():
        wide_ref[:, EDGE + broad :] = jnp.zeros((depth, EDGE, tall), jnp.float32)

    @pl.when(jnp.logical_not(has_west))
    def _():
        next_ref[:, 0:EDGE] = jnp.zeros((depth, EDGE, tall), jnp.float32)
        west_ref[...] = jnp.zeros(west_ref.shape, jnp.float32)

    @pl.when(jnp.logical_not(has_east))
    def _():
        next_ref[:, EDGE + strip :] = jnp.zeros((depth, EDGE, tall), jnp.float32)
        east_ref[...] = jnp.zeros(east_ref.shape, jnp.float32)

    def places(size, part, shape):
        index = lax.broadcasted_iota(jnp.int32, shape, 1)
        plane = jnp.zeros(shape, jnp.int32)
        for z in range(1, depth):
            plane = plane + jnp.where(index >= z * part, 1, 0)
        return plane, index - plane * part

    def build(v, carry):
        @pl.when(v != view)
        def _():
            copy(
                taps_ref.at[v], taps_ref.at[v], tap_send.at[0], tap_recv.at[v], peer(1)[1]
            ).wait_recv()

        table = taps_ref[v]
        x_in = lax.broadcasted_iota(jnp.int32, (span, inner), 0)
        along_x = x_in - places(inner, strip, (span, inner))[1] - (EDGE - HALF)
        band = jnp.zeros((span, inner), jnp.float32)
        for c in range(taps):
            band = jnp.where(along_x == c, table[0:1, c : c + 1], band)
        z_out = places(inner, strip, (1, inner))[0]
        for z in range(depth):
            across = jnp.zeros((1, inner), jnp.float32)
            for c in range(max(0, HALF - depth + 1), min(taps, HALF + depth)):
                across = jnp.where(z - z_out + HALF == c, table[2:3, c : c + 1], across)
            block = band * across
            rows = slice(z * span, (z + 1) * span)
            gt_hi[v, rows], gt_lo[v, rows] = split(block)
            whole_ref[rows] = block
        g_hi[v], g_lo[v] = split(whole_ref[...].T)
        chunk = 64 if tall % 64 == 0 else tall
        for y in range(0, tall, chunk):
            shape = (chunk, tall)
            along_y = (
                lax.broadcasted_iota(jnp.int32, shape, 1)
                - lax.broadcasted_iota(jnp.int32, shape, 0)
                + (HALF - y)
            )
            lines = jnp.zeros(shape, jnp.float32)
            for c in range(taps):
                lines = jnp.where(along_y == c, table[1:2, c : c + 1], lines)
            m_hi[v, y : y + chunk], m_lo[v, y : y + chunk] = split(lines)
        return carry

    lax.fori_loop(0, views, build, 0)

    def over_west(it, v, part):
        planes = pl.ds(part * (depth // parts[it]), depth // parts[it])
        return copy(
            corr_ref.at[it, v, planes, 0:EDGE],
            east_ref.at[it, v, planes],
            over_send.at[it, 0, v, part],
            over_recv.at[it, 0, v, part],
            west_id,
        )

    def over_east(it, v, part):
        planes = pl.ds(part * (depth // parts[it]), depth // parts[it])
        return copy(
            corr_ref.at[it, v, planes, EDGE + strip :],
            west_ref.at[it, v, planes],
            over_send.at[it, 1, v, part],
            over_recv.at[it, 1, v, part],
            east_id,
        )

    def send_over(it, v, part):
        @pl.when(has_west)
        def _():
            over_west(it, v, part).start()

        @pl.when(has_east)
        def _():
            over_east(it, v, part).start()

    def halo_west():
        return copy(
            next_ref.at[:, EDGE : 2 * EDGE],
            next_ref.at[:, EDGE + strip :],
            halo_send.at[0],
            halo_recv.at[0],
            west_id,
        )

    def halo_east():
        return copy(
            next_ref.at[:, strip : EDGE + strip],
            next_ref.at[:, 0:EDGE],
            halo_send.at[1],
            halo_recv.at[1],
            east_id,
        )

    def forward(*vs):
        spread = [product((g_hi[v], g_lo[v]), (p_hi[...], p_lo[...]), (1, 0)) for v in vs]
        return [
            product(split(w), (m_hi[v], m_lo[v]), (1, 1)) for v, w in zip(vs, spread)
        ]

    def gathered(v, blurred):
        ratio = seen_ref[v].reshape(inner, tall) / blurred
        return split(product(split(ratio), (m_hi[v], m_lo[v]), (1, 0)))

    def arrived(it, part):
        def body(v, carry):
            @pl.when(has_east)
            def _():
                over_west(it, v, part).wait_recv()

            @pl.when(has_west)
            def _():
                over_east(it, v, part).wait_recv()

            return carry

        lax.fori_loop(0, views, body, 0)

    def factor(it, z):
        total = jnp.zeros((strip, tall), jnp.float32)
        for v in range(views):
            mid = corr_ref[it, v, z, EDGE : EDGE + strip]
            low = mid[:EDGE] + west_ref[it, v, z]
            high = mid[strip - EDGE :] + east_ref[it, v, z]
            total = total + jnp.log(
                jnp.concatenate([low, mid[EDGE : strip - EDGE], high], axis=0)
            )
        return jnp.exp(total / views)

    @pl.when(tile < tiles - 1)
    def _():
        edge_west().wait_recv()

    @pl.when(tile > 0)
    def _():
        edge_east().wait_recv()

    p_hi[...], p_lo[...] = split(wide_ref[:, pl.ds(first, span)].reshape(outer, tall))

    def ahead(i, carry):
        blur_ref[2 * i], blur_ref[2 * i + 1] = forward(2 * i, 2 * i + 1)
        return carry

    lax.fori_loop(0, views // 2, ahead, 0)

    def first_back(k, carry):
        from_side = jnp.where(k < half, side, 1 - side)
        v = from_side * half + lax.rem(place + k, half)

        @pl.when(v != view)
        def _():
            for z in range(depth):
                copy(
                    flip_ref.at[z, pl.ds(0, strip)],
                    seen_ref.at[v, z],
                    rec_send.at[0, z],
                    rec_recv.at[v, z],
                    peer(1)[1],
                ).wait_recv()

        a = gathered(v, blur_ref[v])
        corr_ref[0, v] = product((gt_hi[v], gt_lo[v]), a, (1, 0)).reshape(depth, span, tall)
        send_over(0, v, 0)
        return carry

    lax.fori_loop(0, views, first_back, 0)
    arrived(0, 0)
    for z in range(depth):
        old = wide_ref[z, pl.ds(pl.multiple_of(first + EDGE, EDGE), strip)]
        next_ref[z, EDGE : EDGE + strip] = old * factor(0, z)

    @pl.when(has_west)
    def _():
        halo_west().start()

    @pl.when(has_east)
    def _():
        halo_east().start()

    @pl.when(has_east)
    def _():
        halo_west().wait_recv()

    @pl.when(has_west)
    def _():
        halo_east().wait_recv()

    p_hi[...], p_lo[...] = split(next_ref[...].reshape(outer, tall))

    planes = depth // parts[1]

    def spread_back(part, *vs):
        rows = slice(part * planes * span, (part + 1) * planes * span)
        for v in vs:
            c = product((gt_hi[v, rows], gt_lo[v, rows]), (a_hi[v], a_lo[v]), (1, 0))
            corr_ref[1, v, part * planes : (part + 1) * planes] = c.reshape(planes, span, tall)
        for v in vs:
            send_over(1, v, part)

    def second(i, carry):
        vs = 2 * i, 2 * i + 1
        for v, blurred in zip(vs, forward(*vs)):
            a_hi[v], a_lo[v] = gathered(v, blurred)
        spread_back(0, *vs)
        return carry

    lax.fori_loop(0, views // 2, second, 0)

    def rest(i, carry):
        spread_back(1, 2 * i, 2 * i + 1)
        return carry

    lax.fori_loop(0, views // 2, rest, 0)

    def out_copy(source, z, way):
        rows = out_ref.at[
            0, z, pl.ds(pl.multiple_of(strip_of(source) * strip, strip), strip)
        ]
        return copy(
            rows,
            rows,
            out_send.at[way, source, z],
            out_recv.at[source, z],
            {"tile": tile, "view": view + 2 * way - 1},
        )

    for z in range(depth):
        if z % planes == 0:
            arrived(1, z // planes)
        out_ref[0, z, pl.ds(first, strip)] = next_ref[z, EDGE : EDGE + strip] * factor(1, z)

        @pl.when(view < views - 1)
        def _():
            out_copy(view, z, 1).start()

        @pl.when(view > 0)
        def _():
            out_copy(view, z, 0).start()

    for distance in range(1, views):
        for z in range(depth):

            @pl.when(view >= distance)
            def _():
                out_copy(view - distance, z, 1).wait_recv()

                @pl.when(view < views - 1)
                def _():
                    out_copy(view - distance, z, 1).start()

            @pl.when(view + distance < views)
            def _():
                out_copy(view + distance, z, 0).wait_recv()

                @pl.when(view > 0)
                def _():
                    out_copy(view + distance, z, 0).start()

    for shift in range(views - 1):
        tap_copy(shift).wait_send()
        for z in range(depth):
            rec_copy(shift, z).wait_send()

    for source in range(views):

        @pl.when((source <= view) & (view < views - 1))
        def _():
            for z in range(depth):
                out_copy(source, z, 1).wait_send()

        @pl.when((source >= view) & (view > 0))
        def _():
            for z in range(depth):
                out_copy(source, z, 0).wait_send()

    @pl.when(tile > 0)
    def _():
        edge_west().wait_send()

    @pl.when(tile < tiles - 1)
    def _():
        edge_east().wait_send()

    @pl.when(has_west)
    def _():
        halo_west().wait_send()
        for it in range(ITERS):
            for v in range(views):
                for part in range(parts[it]):
                    over_west(it, v, part).wait_send()

    @pl.when(has_east)
    def _():
        halo_east().wait_send()
        for it in range(ITERS):
            for v in range(views):
                for part in range(parts[it]):
                    over_east(it, v, part).wait_send()


def by_strips(initial, recorded, tap_table, variants):
    views = lax.axis_size("view")
    depth, tall, broad = initial.shape[1:]
    strip = broad // views
    span = strip + 2 * EDGE
    inner, outer = depth * strip, depth * span
    f32, bf16 = jnp.float32, jnp.bfloat16
    vmem = pl.BlockSpec(memory_space=pltpu.VMEM)
    anywhere = pl.BlockSpec(memory_space=pl.ANY)
    dma = pltpu.SemaphoreType.DMA
    by_axis = jnp.swapaxes(tap_table, 1, 2)
    flipped = pl.pallas_call(
        strips_kernel,
        out_shape=jax.ShapeDtypeStruct((1, depth, broad, tall), f32),
        in_specs=[anywhere, anywhere, anywhere, pl.BlockSpec(memory_space=pltpu.SMEM)],
        out_specs=vmem,
        scratch_shapes=[
            pltpu.VMEM((depth, tall, broad), f32),
            pltpu.VMEM((depth, tall, broad), f32),
            pltpu.VMEM(by_axis.shape[1:], f32),
            pltpu.VMEM((depth, broad + 2 * EDGE, tall), f32),
            pltpu.VMEM((depth, broad, tall), f32),
            pltpu.VMEM((views, depth, strip, tall), f32),
            pltpu.VMEM((views, 8, 128), f32),
            pltpu.VMEM((views, inner, outer), bf16),
            pltpu.VMEM((views, inner, outer), bf16),
            pltpu.VMEM((views, outer, inner), bf16),
            pltpu.VMEM((views, outer, inner), bf16),
            pltpu.VMEM((views, tall, tall), bf16),
            pltpu.VMEM((views, tall, tall), bf16),
            pltpu.VMEM((outer, tall), bf16),
            pltpu.VMEM((outer, tall), bf16),
            pltpu.VMEM((outer, inner), f32),
            pltpu.VMEM((views, inner, tall), bf16),
            pltpu.VMEM((views, inner, tall), bf16),
            pltpu.VMEM((views, inner, tall), f32),
            pltpu.VMEM((ITERS, views, depth, span, tall), f32),
            pltpu.VMEM((ITERS, views, depth, EDGE, tall), f32),
            pltpu.VMEM((ITERS, views, depth, EDGE, tall), f32),
            pltpu.VMEM((depth, span, tall), f32),
            dma((2 + depth,)),
            dma((views - 1,)),
            dma((views,)),
            dma((views - 1, depth)),
            dma((views, depth)),
            dma((2,)),
            dma((2,)),
            dma((ITERS, 2, views, 2)),
            dma((ITERS, 2, views, 2)),
            dma((2,)),
            dma((2,)),
            dma((2, views, depth)),
            dma((views, depth)),
        ],
        compiler_params=pltpu.CompilerParams(
            collective_id=0, has_side_effects=True, vmem_limit_bytes=56 * 2**20
        ),
        name="strips",
    )(initial, recorded, by_axis, variants)
    return jnp.swapaxes(flipped, 2, 3)


def solution(mesh):
    rows_of_tiles = mesh.shape["tile"] // GX
    return jax.shard_map(
        by_strips if rows_of_tiles == 1 else per_device,
        mesh=mesh,
        in_specs=(
            P("tile", None, None, None),
            P("view", "tile", None, None, None),
            P("view", None, None, None),
            P("view", None),
        ),
        out_specs=P("tile", None, None, None),
        check_vma=False,
    )
```

```python
import jax
import jax.numpy as jnp
from jax import lax
from jax.experimental import pallas as pl
from jax.experimental.pallas import tpu as pltpu
from jax.sharding import PartitionSpec as P

GX = 8
ITERS = 2
HALF = 15
EDGE = 16
MESH = pl.DeviceIdType.MESH


def passed_along(block, axis, distance):
    devices = range(lax.axis_size(axis))
    route = [(i - distance, i) for i in devices if i - distance in devices]
    return lax.ppermute(block, axis, route)


def normalized(tap_table):
    return tap_table / jnp.sum(tap_table, axis=-1, keepdims=True)


def tile_kernels(kernels, variant_ids, grid_rows, grid_cols):
    count_variants = kernels.shape[0]
    onehot = (variant_ids[:, None] == jnp.arange(count_variants, dtype=jnp.int32)[None, :]).astype(
        jnp.float32
    )
    flat = jnp.dot(onehot, kernels.reshape(count_variants, -1), precision=lax.Precision.HIGHEST)
    return flat.reshape(grid_rows, grid_cols, 3, kernels.shape[-1])


def tile_onehot(positions, extent, count):
    owner = jnp.clip(jnp.floor_divide(positions, extent), 0, count - 1)
    return (owner[:, None] == jnp.arange(count, dtype=jnp.int32)[None, :]).astype(jnp.float32)


def weight_map(tile_taps, axis_id, offset, row_hot, col_hot):
    inner = jnp.dot(row_hot, tile_taps[:, :, axis_id, offset], precision=lax.Precision.HIGHEST)
    return jnp.dot(inner, col_hot.T, precision=lax.Precision.HIGHEST)


def blur_cols(padded, tile_taps, row_hot, col_hot):
    count = col_hot.shape[0]
    result = jnp.zeros((padded.shape[0], padded.shape[1], count), jnp.float32)
    for offset in range(tile_taps.shape[3]):
        weights = weight_map(tile_taps, 0, offset, row_hot, col_hot)
        result = result + weights[None] * padded[:, :, offset : offset + count]
    return result


def blur_rows(padded, tile_taps, row_hot, col_hot):
    count = row_hot.shape[0]
    result = jnp.zeros((padded.shape[0], count, padded.shape[2]), jnp.float32)
    for offset in range(tile_taps.shape[3]):
        weights = weight_map(tile_taps, 1, offset, row_hot, col_hot)
        result = result + weights[None] * padded[:, offset : offset + count, :]
    return result


def blur_planes(field, tile_taps, row_hot, col_hot, reverse):
    taps = tile_taps.shape[3]
    margin = taps // 2
    padded = jnp.pad(field, ((margin, margin), (0, 0), (0, 0)))
    planes = field.shape[0]
    result = jnp.zeros(field.shape, jnp.float32)
    for offset in range(taps):
        which = taps - 1 - offset if reverse else offset
        weights = weight_map(tile_taps, 2, which, row_hot, col_hot)
        result = result + weights[None] * padded[offset : offset + planes]
    return result


def adjoint_rows(padded, tile_taps, row_hot, col_hot):
    margin = tile_taps.shape[3] // 2
    count = padded.shape[1] - 2 * margin
    result = jnp.zeros((padded.shape[0], count, padded.shape[2]), jnp.float32)
    for offset in range(tile_taps.shape[3]):
        lead = 2 * margin - offset
        weights = weight_map(tile_taps, 1, offset, row_hot, col_hot)
        result = result + weights[None, lead : lead + count, :] * padded[:, lead : lead + count, :]
    return result


def adjoint_cols(padded, tile_taps, row_hot, col_hot):
    margin = tile_taps.shape[3] // 2
    count = padded.shape[2] - 2 * margin
    result = jnp.zeros((padded.shape[0], padded.shape[1], count), jnp.float32)
    for offset in range(tile_taps.shape[3]):
        lead = 2 * margin - offset
        weights = weight_map(tile_taps, 0, offset, row_hot, col_hot)
        result = result + weights[None, :, lead : lead + count] * padded[:, :, lead : lead + count]
    return result


def widen_cols(field, width, tile_col):
    west_send = field[:, :, -width:]
    east_send = field[:, :, :width]
    west_send = jnp.where(tile_col < GX - 1, west_send, jnp.zeros_like(west_send))
    east_send = jnp.where(tile_col > 0, east_send, jnp.zeros_like(east_send))
    from_west = passed_along(west_send, "tile", 1)
    from_east = passed_along(east_send, "tile", -1)
    return jnp.concatenate([from_west, field, from_east], axis=2)


def widen_rows(field, width):
    from_north = passed_along(field[:, -width:, :], "tile", GX)
    from_south = passed_along(field[:, :width, :], "tile", -GX)
    return jnp.concatenate([from_north, field, from_south], axis=1)


def per_device(initial, recorded, tap_table, variants):
    position = lax.axis_index("tile")
    count_tiles = lax.axis_size("tile")
    count_views = lax.axis_size("view")
    grid_rows = count_tiles // GX
    tile_row = position // GX
    tile_col = position % GX
    tile_taps = tile_kernels(normalized(tap_table[0]), variants[0], grid_rows, GX)
    estimate = initial[0]
    observed = recorded[0, 0]
    tall = estimate.shape[1]
    broad = estimate.shape[2]
    row_first = tile_row * tall
    col_first = tile_col * broad

    def row_places(margin):
        return row_first + jnp.arange(tall + 2 * margin, dtype=jnp.int32) - margin

    def col_places(margin):
        return col_first + jnp.arange(broad + 2 * margin, dtype=jnp.int32) - margin

    own_rows = tile_onehot(row_places(0), tall, grid_rows)
    own_cols = tile_onehot(col_places(0), broad, GX)
    wide_rows = tile_onehot(row_places(HALF), tall, grid_rows)
    wide_cols = tile_onehot(col_places(HALF), broad, GX)
    for step in range(ITERS):
        padded = widen_cols(estimate, HALF, tile_col)
        planes = blur_planes(
            blur_cols(padded, tile_taps, own_rows, own_cols), tile_taps, own_rows, own_cols, False
        )
        blurred = blur_rows(widen_rows(planes, HALF), tile_taps, own_rows, own_cols)
        ratio = observed / blurred
        back = adjoint_rows(widen_rows(ratio, HALF), tile_taps, wide_rows, own_cols)
        back = blur_planes(back, tile_taps, own_rows, own_cols, True)
        correction = adjoint_cols(widen_cols(back, HALF, tile_col), tile_taps, own_rows, wide_cols)
        logged = jnp.log(correction)
        summed = lax.psum(logged, "view")
        estimate = estimate * jnp.exp(summed / count_views)
    return estimate[None]


def split(value):
    high = value.astype(jnp.bfloat16)
    return high, (value - high.astype(jnp.float32)).astype(jnp.bfloat16)


def product(left, right, contract):
    dims = (((contract[0],), (contract[1],)), ((), ()))

    def one(a, b):
        return lax.dot_general(a, b, dims, preferred_element_type=jnp.float32)

    return one(left[0], right[0]) + (one(left[0], right[1]) + one(left[1], right[0]))


def strips_kernel(
    init_hbm,
    rec_hbm,
    tap_hbm,
    var_ref,
    out_ref,
    init_ref,
    rec_ref,
    tap_ref,
    wide_ref,
    flip_ref,
    seen_ref,
    taps_ref,
    g_hi,
    g_lo,
    gt_hi,
    gt_lo,
    m_hi,
    m_lo,
    p_hi,
    p_lo,
    whole_ref,
    a_hi,
    a_lo,
    blur_ref,
    corr_ref,
    west_ref,
    east_ref,
    next_ref,
    load_sem,
    tap_send,
    tap_recv,
    rec_send,
    rec_recv,
    edge_send,
    edge_recv,
    over_send,
    over_recv,
    halo_send,
    halo_recv,
    out_send,
    out_recv,
):
    tile = lax.axis_index("tile")
    view = lax.axis_index("view")
    tiles = lax.axis_size("tile")
    views = lax.axis_size("view")
    depth, tall, broad = init_ref.shape
    strip = broad // views
    span = strip + 2 * EDGE
    inner, outer = depth * strip, depth * span
    taps = tap_ref.shape[2]
    parts = (1, 2)

    tap_load = pltpu.make_async_copy(tap_hbm.at[0], tap_ref, load_sem.at[0])
    init_load = pltpu.make_async_copy(init_hbm.at[0], init_ref, load_sem.at[1])
    rec_loads = [
        pltpu.make_async_copy(rec_hbm.at[0, 0, z], rec_ref.at[z], load_sem.at[2 + z])
        for z in range(depth)
    ]
    tap_load.start()
    for z in range(depth):
        rec_loads[z].start()
    init_load.start()

    def strip_of(position):
        odd = lax.rem(tile, 2)
        return position + odd * (views - 1 - 2 * position)

    mine = strip_of(view)
    has_west = (tile > 0) | (mine > 0)
    has_east = (tile < tiles - 1) | (mine < views - 1)
    step = 1 - 2 * lax.rem(tile, 2)
    west_id = {
        "tile": jnp.where(mine > 0, tile, tile - 1),
        "view": jnp.where(mine > 0, view - step, view),
    }
    east_id = {
        "tile": jnp.where(mine < views - 1, tile, tile + 1),
        "view": jnp.where(mine < views - 1, view + step, view),
    }
    first = pl.multiple_of(mine * strip, strip)

    half = views // 2
    side, place = view // half, lax.rem(view, half)

    def peer(order):
        if order < half:
            other = (1 - side) * half + lax.rem(place + order, half)
        else:
            other = side * half + lax.rem(place + order - half + 1, half)
        return other, {"tile": tile, "view": other}

    def copy(source, target, send, recv, device):
        return pltpu.make_async_remote_copy(
            src_ref=source,
            dst_ref=target,
            send_sem=send,
            recv_sem=recv,
            device_id=device,
            device_id_type=MESH,
        )

    barrier = pltpu.get_barrier_semaphore()
    for shift in range(views - 1):
        pl.semaphore_signal(barrier, inc=1, device_id=peer(shift)[1], device_id_type=MESH)

    @pl.when(tile > 0)
    def _():
        pl.semaphore_signal(
            barrier, inc=1, device_id={"tile": tile - 1, "view": view}, device_id_type=MESH
        )

    @pl.when(tile < tiles - 1)
    def _():
        pl.semaphore_signal(
            barrier, inc=1, device_id={"tile": tile + 1, "view": view}, device_id_type=MESH
        )

    tap_load.wait()
    chosen = lax.broadcasted_iota(jnp.int32, tap_ref.shape[1:], 0) == var_ref[0, tile]
    taps_ref[view] = jnp.zeros(taps_ref.shape[1:], jnp.float32)
    for a in range(tap_ref.shape[0]):
        own_taps = jnp.sum(jnp.where(chosen, tap_ref[a], 0.0), axis=0, keepdims=True)
        own_taps = own_taps / jnp.sum(own_taps, axis=-1, keepdims=True)
        taps_ref[view, a : a + 1, 0:taps] = own_taps
    rec_loads[0].wait()
    flip_ref[0] = rec_ref[0].T

    pl.semaphore_wait(
        barrier, views - 1 + jnp.where(tile > 0, 1, 0) + jnp.where(tile < tiles - 1, 1, 0)
    )

    def tap_copy(shift):
        return copy(
            taps_ref.at[view],
            taps_ref.at[view],
            tap_send.at[shift],
            tap_recv.at[view],
            peer(shift)[1],
        )

    for shift in range(views - 1):
        tap_copy(shift).start()

    def rec_copy(shift, z):
        other, device = peer(shift)
        rows = pl.ds(pl.multiple_of(strip_of(other) * strip, strip), strip)
        return copy(
            flip_ref.at[z, rows],
            seen_ref.at[view, z],
            rec_send.at[shift, z],
            rec_recv.at[view, z],
            device,
        )

    for z in range(depth):
        if z > 0:
            rec_loads[z].wait()
            flip_ref[z] = rec_ref[z].T
        rec_copy(0, z).start()
        seen_ref[view, z] = flip_ref[z, pl.ds(first, strip)]

    for shift in range(1, views - 1):
        for z in range(depth):
            rec_copy(shift, z).start()

    init_load.wait()
    for z in range(depth):
        wide_ref[z, EDGE : EDGE + broad] = init_ref[z].T

    def edge_west():
        return copy(
            wide_ref.at[:, EDGE : 2 * EDGE],
            wide_ref.at[:, EDGE + broad :],
            edge_send.at[0],
            edge_recv.at[0],
            {"tile": tile - 1, "view": view},
        )

    def edge_east():
        return copy(
            wide_ref.at[:, broad : EDGE + broad],
            wide_ref.at[:, 0:EDGE],
            edge_send.at[1],
            edge_recv.at[1],
            {"tile": tile + 1, "view": view},
        )

    @pl.when(tile > 0)
    def _():
        edge_west().start()

    @pl.when(tile < tiles - 1)
    def _():
        edge_east().start()

    @pl.when(tile == 0)
    def _():
        wide_ref[:, 0:EDGE] = jnp.zeros((depth, EDGE, tall), jnp.float32)

    @pl.when(tile == tiles - 1)
    def _():
        wide_ref[:, EDGE + broad :] = jnp.zeros((depth, EDGE, tall), jnp.float32)

    @pl.when(jnp.logical_not(has_west))
    def _():
        next_ref[:, 0:EDGE] = jnp.zeros((depth, EDGE, tall), jnp.float32)
        west_ref[...] = jnp.zeros(west_ref.shape, jnp.float32)

    @pl.when(jnp.logical_not(has_east))
    def _():
        next_ref[:, EDGE + strip :] = jnp.zeros((depth, EDGE, tall), jnp.float32)
        east_ref[...] = jnp.zeros(east_ref.shape, jnp.float32)

    def places(size, part, shape):
        index = lax.broadcasted_iota(jnp.int32, shape, 1)
        plane = jnp.zeros(shape, jnp.int32)
        for z in range(1, depth):
            plane = plane + jnp.where(index >= z * part, 1, 0)
        return plane, index - plane * part

    def build(v, carry):
        @pl.when(v != view)
        def _():
            copy(
                taps_ref.at[v], taps_ref.at[v], tap_send.at[0], tap_recv.at[v], peer(1)[1]
            ).wait_recv()

        table = taps_ref[v]
        x_in = lax.broadcasted_iota(jnp.int32, (span, inner), 0)
        along_x = x_in - places(inner, strip, (span, inner))[1] - (EDGE - HALF)
        band = jnp.zeros((span, inner), jnp.float32)
        for c in range(taps):
            band = jnp.where(along_x == c, table[0:1, c : c + 1], band)
        z_out = places(inner, strip, (1, inner))[0]
        for z in range(depth):
            across = jnp.zeros((1, inner), jnp.float32)
            for c in range(max(0, HALF - depth + 1), min(taps, HALF + depth)):
                across = jnp.where(z - z_out + HALF == c, table[2:3, c : c + 1], across)
            block = band * across
            rows = slice(z * span, (z + 1) * span)
            gt_hi[v, rows], gt_lo[v, rows] = split(block)
            whole_ref[rows] = block
        g_hi[v], g_lo[v] = split(whole_ref[...].T)
        chunk = 64 if tall % 64 == 0 else tall
        for y in range(0, tall, chunk):
            shape = (chunk, tall)
            along_y = (
                lax.broadcasted_iota(jnp.int32, shape, 1)
                - lax.broadcasted_iota(jnp.int32, shape, 0)
                + (HALF - y)
            )
            lines = jnp.zeros(shape, jnp.float32)
            for c in range(taps):
                lines = jnp.where(along_y == c, table[1:2, c : c + 1], lines)
            m_hi[v, y : y + chunk], m_lo[v, y : y + chunk] = split(lines)
        return carry

    lax.fori_loop(0, views, build, 0)

    def over_west(it, v, part):
        planes = pl.ds(part * (depth // parts[it]), depth // parts[it])
        return copy(
            corr_ref.at[it, v, planes, 0:EDGE],
            east_ref.at[it, v, planes],
            over_send.at[it, 0, v, part],
            over_recv.at[it, 0, v, part],
            west_id,
        )

    def over_east(it, v, part):
        planes = pl.ds(part * (depth // parts[it]), depth // parts[it])
        return copy(
            corr_ref.at[it, v, planes, EDGE + strip :],
            west_ref.at[it, v, planes],
            over_send.at[it, 1, v, part],
            over_recv.at[it, 1, v, part],
            east_id,
        )

    def send_over(it, v, part):
        @pl.when(has_west)
        def _():
            over_west(it, v, part).start()

        @pl.when(has_east)
        def _():
            over_east(it, v, part).start()

    def halo_west():
        return copy(
            next_ref.at[:, EDGE : 2 * EDGE],
            next_ref.at[:, EDGE + strip :],
            halo_send.at[0],
            halo_recv.at[0],
            west_id,
        )

    def halo_east():
        return copy(
            next_ref.at[:, strip : EDGE + strip],
            next_ref.at[:, 0:EDGE],
            halo_send.at[1],
            halo_recv.at[1],
            east_id,
        )

    def forward(*vs):
        spread = [product((g_hi[v], g_lo[v]), (p_hi[...], p_lo[...]), (1, 0)) for v in vs]
        return [
            product(split(w), (m_hi[v], m_lo[v]), (1, 1)) for v, w in zip(vs, spread)
        ]

    def gathered(v, blurred):
        ratio = seen_ref[v].reshape(inner, tall) / blurred
        return split(product(split(ratio), (m_hi[v], m_lo[v]), (1, 0)))

    def arrived(it, part):
        def body(v, carry):
            @pl.when(has_east)
            def _():
                over_west(it, v, part).wait_recv()

            @pl.when(has_west)
            def _():
                over_east(it, v, part).wait_recv()

            return carry

        lax.fori_loop(0, views, body, 0)

    def factor(it, z):
        total = jnp.zeros((strip, tall), jnp.float32)
        for v in range(views):
            mid = corr_ref[it, v, z, EDGE : EDGE + strip]
            low = mid[:EDGE] + west_ref[it, v, z]
            high = mid[strip - EDGE :] + east_ref[it, v, z]
            total = total + jnp.log(
                jnp.concatenate([low, mid[EDGE : strip - EDGE], high], axis=0)
            )
        return jnp.exp(total / views)

    @pl.when(tile < tiles - 1)
    def _():
        edge_west().wait_recv()

    @pl.when(tile > 0)
    def _():
        edge_east().wait_recv()

    p_hi[...], p_lo[...] = split(wide_ref[:, pl.ds(first, span)].reshape(outer, tall))

    def ahead(i, carry):
        blur_ref[2 * i], blur_ref[2 * i + 1] = forward(2 * i, 2 * i + 1)
        return carry

    lax.fori_loop(0, views // 2, ahead, 0)

    def first_back(k, carry):
        from_side = jnp.where(k < half, side, 1 - side)
        v = from_side * half + lax.rem(place + k, half)

        @pl.when(v != view)
        def _():
            for z in range(depth):
                copy(
                    flip_ref.at[z, pl.ds(0, strip)],
                    seen_ref.at[v, z],
                    rec_send.at[0, z],
                    rec_recv.at[v, z],
                    peer(1)[1],
                ).wait_recv()

        a = gathered(v, blur_ref[v])
        corr_ref[0, v] = product((gt_hi[v], gt_lo[v]), a, (1, 0)).reshape(depth, span, tall)
        send_over(0, v, 0)
        return carry

    lax.fori_loop(0, views, first_back, 0)
    arrived(0, 0)
    for z in range(depth):
        old = wide_ref[z, pl.ds(pl.multiple_of(first + EDGE, EDGE), strip)]
        next_ref[z, EDGE : EDGE + strip] = old * factor(0, z)

    @pl.when(has_west)
    def _():
        halo_west().start()

    @pl.when(has_east)
    def _():
        halo_east().start()

    @pl.when(has_east)
    def _():
        halo_west().wait_recv()

    @pl.when(has_west)
    def _():
        halo_east().wait_recv()

    p_hi[...], p_lo[...] = split(next_ref[...].reshape(outer, tall))

    planes = depth // parts[1]

    def spread_back(part, *vs):
        rows = slice(part * planes * span, (part + 1) * planes * span)
        for v in vs:
            c = product((gt_hi[v, rows], gt_lo[v, rows]), (a_hi[v], a_lo[v]), (1, 0))
            corr_ref[1, v, part * planes : (part + 1) * planes] = c.reshape(planes, span, tall)
        for v in vs:
            send_over(1, v, part)

    def second(i, carry):
        vs = 2 * i, 2 * i + 1
        for v, blurred in zip(vs, forward(*vs)):
            a_hi[v], a_lo[v] = gathered(v, blurred)
        spread_back(0, *vs)
        return carry

    lax.fori_loop(0, views // 2, second, 0)

    def rest(i, carry):
        spread_back(1, 2 * i, 2 * i + 1)
        return carry

    lax.fori_loop(0, views // 2, rest, 0)

    def out_copy(source, z, way):
        rows = out_ref.at[
            0, z, pl.ds(pl.multiple_of(strip_of(source) * strip, strip), strip)
        ]
        return copy(
            rows,
            rows,
            out_send.at[way, source, z],
            out_recv.at[source, z],
            {"tile": tile, "view": view + 2 * way - 1},
        )

    for z in range(depth):
        if z % planes == 0:
            arrived(1, z // planes)
        out_ref[0, z, pl.ds(first, strip)] = next_ref[z, EDGE : EDGE + strip] * factor(1, z)

        @pl.when(view < views - 1)
        def _():
            out_copy(view, z, 1).start()

        @pl.when(view > 0)
        def _():
            out_copy(view, z, 0).start()

    for distance in range(1, views):
        for z in range(depth):

            @pl.when(view >= distance)
            def _():
                out_copy(view - distance, z, 1).wait_recv()

                @pl.when(view < views - 1)
                def _():
                    out_copy(view - distance, z, 1).start()

            @pl.when(view + distance < views)
            def _():
                out_copy(view + distance, z, 0).wait_recv()

                @pl.when(view > 0)
                def _():
                    out_copy(view + distance, z, 0).start()

    for shift in range(views - 1):
        tap_copy(shift).wait_send()
        for z in range(depth):
            rec_copy(shift, z).wait_send()

    for source in range(views):

        @pl.when((source <= view) & (view < views - 1))
        def _():
            for z in range(depth):
                out_copy(source, z, 1).wait_send()

        @pl.when((source >= view) & (view > 0))
        def _():
            for z in range(depth):
                out_copy(source, z, 0).wait_send()

    @pl.when(tile > 0)
    def _():
        edge_west().wait_send()

    @pl.when(tile < tiles - 1)
    def _():
        edge_east().wait_send()

    @pl.when(has_west)
    def _():
        halo_west().wait_send()
        for it in range(ITERS):
            for v in range(views):
                for part in range(parts[it]):
                    over_west(it, v, part).wait_send()

    @pl.when(has_east)
    def _():
        halo_east().wait_send()
        for it in range(ITERS):
            for v in range(views):
                for part in range(parts[it]):
                    over_east(it, v, part).wait_send()


def by_strips(initial, recorded, tap_table, variants):
    views = lax.axis_size("view")
    depth, tall, broad = initial.shape[1:]
    strip = broad // views
    span = strip + 2 * EDGE
    inner, outer = depth * strip, depth * span
    f32, bf16 = jnp.float32, jnp.bfloat16
    vmem = pl.BlockSpec(memory_space=pltpu.VMEM)
    anywhere = pl.BlockSpec(memory_space=pl.ANY)
    dma = pltpu.SemaphoreType.DMA
    by_axis = jnp.swapaxes(tap_table, 1, 2)
    flipped = pl.pallas_call(
        strips_kernel,
        out_shape=jax.ShapeDtypeStruct((1, depth, broad, tall), f32),
        in_specs=[anywhere, anywhere, anywhere, pl.BlockSpec(memory_space=pltpu.SMEM)],
        out_specs=vmem,
        scratch_shapes=[
            pltpu.VMEM((depth, tall, broad), f32),
            pltpu.VMEM((depth, tall, broad), f32),
            pltpu.VMEM(by_axis.shape[1:], f32),
            pltpu.VMEM((depth, broad + 2 * EDGE, tall), f32),
            pltpu.VMEM((depth, broad, tall), f32),
            pltpu.VMEM((views, depth, strip, tall), f32),
            pltpu.VMEM((views, 8, 128), f32),
            pltpu.VMEM((views, inner, outer), bf16),
            pltpu.VMEM((views, inner, outer), bf16),
            pltpu.VMEM((views, outer, inner), bf16),
            pltpu.VMEM((views, outer, inner), bf16),
            pltpu.VMEM((views, tall, tall), bf16),
            pltpu.VMEM((views, tall, tall), bf16),
            pltpu.VMEM((outer, tall), bf16),
            pltpu.VMEM((outer, tall), bf16),
            pltpu.VMEM((outer, inner), f32),
            pltpu.VMEM((views, inner, tall), bf16),
            pltpu.VMEM((views, inner, tall), bf16),
            pltpu.VMEM((views, inner, tall), f32),
            pltpu.VMEM((ITERS, views, depth, span, tall), f32),
            pltpu.VMEM((ITERS, views, depth, EDGE, tall), f32),
            pltpu.VMEM((ITERS, views, depth, EDGE, tall), f32),
            pltpu.VMEM((depth, span, tall), f32),
            dma((2 + depth,)),
            dma((views - 1,)),
            dma((views,)),
            dma((views - 1, depth)),
            dma((views, depth)),
            dma((2,)),
            dma((2,)),
            dma((ITERS, 2, views, 2)),
            dma((ITERS, 2, views, 2)),
            dma((2,)),
            dma((2,)),
            dma((2, views, depth)),
            dma((views, depth)),
        ],
        compiler_params=pltpu.CompilerParams(
            collective_id=0, has_side_effects=True, vmem_limit_bytes=52 * 2**20
        ),
        name="strips",
    )(initial, recorded, by_axis, variants)
    return jnp.swapaxes(flipped, 2, 3)


def solution(mesh):
    rows_of_tiles = mesh.shape["tile"] // GX
    return jax.shard_map(
        by_strips if rows_of_tiles == 1 else per_device,
        mesh=mesh,
        in_specs=(
            P("tile", None, None, None),
            P("view", "tile", None, None, None),
            P("view", None, None, None),
            P("view", None),
        ),
        out_specs=P("tile", None, None, None),
        check_vma=False,
    )
```
